128 devices in a mesh: energy: 16 (over z, x_hi, core), momentum: 8 (over y, x_lo).
Axes of the slice: x: 4 (x_hi: 2, x_lo: 2; x = x_hi * 2 + x_lo), y: 4, z: 4, core: 2. Of those that a mesh axis runs over, the one named last changes fastest.
Arguments:
- hopping: float32 [8, 2, 2, 384, 384], P('momentum'), may hold values from -0.07 to 0.07, as said below
- coupling: float32 [8, 2, 384, 384], P('momentum'), may hold values from -0.15 to 0.15
- onsite: float32 [2, 384], replicated, may hold values from -4 to -2.5
- sigma_in: float32 [16, 8, 2, 147456], P('energy', 'momentum'), may hold values from -0.12 to 0.12
- neighbor_shift: int32 [96, 48], replicated, may hold values from 1 to 95
- mode_shift: int32 [6], replicated, may hold values from 1 to 7
- phonon_kernel: float32 [6, 2, 8, 8], replicated, may hold values from -240 to 240
Outputs:
- sigma_new: float32 [16, 8, 2, 147456], P('energy', 'momentum')
The draws below stay inside these ranges and needn't reach their ends.
Inputs may be any that keep to these rules, and one draw needn't show every extreme that they name: hopping[k, c, 0] is symmetric with a zero diagonal and hopping[k, c, 1] is antisymmetric, so every cell block is Hermitian.
All inputs are finite; a program needn't handle non-finite values.
Results may differ from the reference program's by a relative error of at most 0.0003.
Values sent between devices are 32-bit elements; how exact they have to be, the bound alone decides.
No kernel may reach another device: no remote copies, remote signals or barrier semaphores. Data moves between devices by JAX's collectives and lax.ppermute only.
A program may use at most 256 MiB of HBM per device.

```python
import jax
import jax.numpy as jnp
from jax import lax

ORB = 384
ORB_ATOM = 4
ATOMS = 96
NEIGH = 48
PAIR_COLS = 147456
MODES = 6
NS_STEPS = 2
ENERGIES = 16
MOMENTA = 8


def draw_hopping(key, part):
    first_key, second_key = jax.random.split(jax.random.fold_in(key, 11))
    array_shape = (MOMENTA, 2, ORB, ORB)
    real_draw = jax.random.uniform(first_key, array_shape, jnp.float32, -0.07, 0.07)
    imag_draw = jax.random.uniform(second_key, array_shape, jnp.float32, -0.07, 0.07)
    row_index = lax.broadcasted_iota(jnp.int32, (ORB, ORB), 0)
    col_index = lax.broadcasted_iota(jnp.int32, (ORB, ORB), 1)
    off_diagonal = (row_index != col_index).astype(jnp.float32)
    real_part = 0.5 * (real_draw + jnp.swapaxes(real_draw, -1, -2)) * off_diagonal
    imag_part = 0.5 * (imag_draw - jnp.swapaxes(imag_draw, -1, -2))
    return jnp.stack([real_part, imag_part], axis=2)


def draw_coupling(key, part):
    first_key = jax.random.fold_in(jax.random.fold_in(key, 23), 0)
    array_shape = (MOMENTA, 2, ORB, ORB)
    entries = 0.025 * jax.random.normal(first_key, array_shape, jnp.float32)
    return jnp.clip(entries, -0.15, 0.15)


def place_ends(array, key, low, high):
    shape = array.shape
    spot = [jax.random.randint(jax.random.fold_in(key, axis), (), 0, shape[axis]) for axis in range(len(shape))]
    array = array.at[tuple(spot)].set(low)
    longest = shape.index(max(shape))
    spot[longest] = (spot[longest] + 1) % shape[longest]
    return array.at[tuple(spot)].set(high)


def block_scale(rng, shape, pieces, smallest, largest):
    def one(position, parts):
        steps = jax.random.uniform(jax.random.fold_in(jax.random.fold_in(rng, 6), position), (parts,), jnp.float32, smallest / len(pieces), largest / len(pieces))
        return jnp.repeat(jnp.exp(steps), shape[position] // parts).reshape((-1,) + (1,) * (len(shape) - position - 1))

    loudness = one(*pieces[0])
    for cut in pieces[1:]:
        loudness = loudness * one(*cut)
    return loudness


def centred(key, shape, deviation, limit, cuts=(), kind=jnp.bfloat16):
    level = block_scale(key, shape, cuts, -0.22, 0.18) if cuts else 1.0
    result = jax.random.normal(key, shape, jnp.float32) * deviation * level
    return jnp.minimum(jnp.maximum(result, -limit), limit).astype(kind)


def setup_inputs(seed: int = 0) -> dict:
    key_of = jax.random.split(jax.random.key(seed), 8)
    return {
        "hopping": draw_hopping(jax.random.fold_in(key_of[7], 71), 0),
        "coupling": draw_coupling(jax.random.fold_in(key_of[7], 71), 0),
        "onsite": jnp.clip(jax.random.uniform(key_of[2], (2, ORB), jnp.float32, -4.0, -2.5), -4.0, -2.5),
        "sigma_in": centred(key_of[3], (ENERGIES, MOMENTA, 2, PAIR_COLS), 0.02, 0.12, ((0, 16), (1, 8)), jnp.float32),
        "neighbor_shift": place_ends(jax.random.randint(key_of[4], (ATOMS, NEIGH), 1, ATOMS), jax.random.fold_in(key_of[4], 1), 1, ATOMS - 1).astype(jnp.int32),
        "mode_shift": place_ends(jax.random.randint(key_of[5], (MODES,), 1, ENERGIES // 2), jax.random.fold_in(key_of[5], 1), 1, (ENERGIES // 2) - 1).astype(jnp.int32),
        "phonon_kernel": centred(key_of[6], (MODES, 2, MOMENTA, MOMENTA), 40.0, 240.0, (), jnp.float32),
    }


BROADENING = 0.5


def matmul_high(first_matrix, second_matrix):
    return jnp.dot(first_matrix, second_matrix, precision=lax.Precision.HIGHEST, preferred_element_type=jnp.float32)


def complex_product(first_pair, second_pair):
    real_real = matmul_high(first_pair[0], second_pair[0])
    imag_imag = matmul_high(first_pair[1], second_pair[1])
    summed = matmul_high(first_pair[0] + first_pair[1], second_pair[0] + second_pair[1])
    return (real_real - imag_imag, summed - real_real - imag_imag)


def newton_inverse(system):
    diagonal_real = jnp.diagonal(system[0])
    diagonal_imag = jnp.diagonal(system[1])
    magnitude = diagonal_real * diagonal_real + diagonal_imag * diagonal_imag
    inverse_real = diagonal_real / magnitude
    inverse_imag = -diagonal_imag / magnitude
    column_real = system[0] * inverse_real[None, :] - system[1] * inverse_imag[None, :]
    column_imag = system[0] * inverse_imag[None, :] + system[1] * inverse_real[None, :]
    scaled_real = inverse_real[:, None] * column_real - inverse_imag[:, None] * column_imag
    scaled_imag = inverse_real[:, None] * column_imag + inverse_imag[:, None] * column_real
    guess = (2.0 * jnp.diag(inverse_real) - scaled_real, 2.0 * jnp.diag(inverse_imag) - scaled_imag)
    for step_number in range(NS_STEPS - 1):
        product = complex_product(system, guess)
        correction = complex_product(guess, product)
        guess = (2.0 * guess[0] - correction[0], 2.0 * guess[1] - correction[1])
    return guess


def place_pairs(pair_values, row_atom, col_atom):
    entries = pair_values.reshape(ATOMS, NEIGH, 2, ORB_ATOM, ORB_ATOM)
    placed = jnp.zeros((2, ATOMS, ORB_ATOM, ATOMS, ORB_ATOM), jnp.float32).at[:, row_atom, :, col_atom, :].add(entries)
    placed = placed.reshape(2, ORB, ORB)
    return (placed[0], placed[1])


def pick_pairs(matrix_pair, row_atom, col_atom):
    stacked = jnp.stack([matrix_pair[0], matrix_pair[1]]).reshape(2, ATOMS, ORB_ATOM, ATOMS, ORB_ATOM)
    return stacked[:, row_atom, :, col_atom, :].reshape(PAIR_COLS)


def green_point(energy_real, hopping_block, coupling_block, onsite, sigma_point, row_atom, col_atom):
    identity = jnp.eye(ORB, dtype=jnp.float32)
    systems = []
    for cell_index in range(2):
        self_energy = place_pairs(sigma_point[cell_index], row_atom, col_atom)
        system_real = jnp.diag(energy_real - onsite[cell_index]) - hopping_block[cell_index, 0] - self_energy[0]
        system_imag = BROADENING * identity - hopping_block[cell_index, 1] - self_energy[1]
        systems.append((system_real, system_imag))
    first_green = newton_inverse(systems[0])
    coupling_pair = (coupling_block[0], coupling_block[1])
    coupling_adjoint = (coupling_block[0].T, -coupling_block[1].T)
    adjoint_green = complex_product(coupling_adjoint, first_green)
    folded = complex_product(adjoint_green, coupling_pair)
    second_green = newton_inverse((systems[1][0] - folded[0], systems[1][1] - folded[1]))
    green_coupling = complex_product(first_green, coupling_pair)
    through = complex_product(complex_product(green_coupling, second_green), adjoint_green)
    first_full = (first_green[0] + through[0], first_green[1] + through[1])
    return jnp.stack([pick_pairs(first_full, row_atom, col_atom), pick_pairs(second_green, row_atom, col_atom)])


def build_kernel(mode_shift, phonon_kernel, energies, momenta):
    target = lax.broadcasted_iota(jnp.int32, (MODES, energies, energies), 1)
    source = lax.broadcasted_iota(jnp.int32, (MODES, energies, energies), 2)
    shifted = mode_shift[:, None, None]
    lower = (source == target - shifted).astype(jnp.float32)
    upper = (source == target + shifted).astype(jnp.float32)
    combined = jnp.einsum("jab,jkq->akbq", lower, phonon_kernel[:, 0], precision=lax.Precision.HIGHEST)
    combined = combined + jnp.einsum("jab,jkq->akbq", upper, phonon_kernel[:, 1], precision=lax.Precision.HIGHEST)
    return combined.reshape(energies * momenta, energies * momenta)


def reference(hopping, coupling, onsite, sigma_in, neighbor_shift, mode_shift, phonon_kernel):
    row_atom = lax.broadcasted_iota(jnp.int32, (ATOMS, NEIGH), 0)
    col_atom = (row_atom + neighbor_shift) % ATOMS

    def one_point(point_index):
        energy = point_index // MOMENTA
        momentum = point_index % MOMENTA
        energy_real = 2.0 * (energy.astype(jnp.float32) + 0.5) / ENERGIES
        return green_point(energy_real, hopping[momentum], coupling[momentum], onsite, sigma_in[energy, momentum], row_atom, col_atom)

    green_pairs = lax.map(one_point, jnp.arange(ENERGIES * MOMENTA, dtype=jnp.int32))
    kernel = build_kernel(mode_shift, phonon_kernel, ENERGIES, MOMENTA)
    flattened = green_pairs.reshape(ENERGIES * MOMENTA, 2 * PAIR_COLS)
    return matmul_high(kernel, flattened).reshape(ENERGIES, MOMENTA, 2, PAIR_COLS)
```

```python
import jax
import jax.numpy as jnp
from jax import lax
from jax.experimental import pallas as pl
from jax.experimental.pallas import tpu as pltpu
from jax.sharding import PartitionSpec as P

ORB = 384
ATOMS = 96
NEIGH = 48
PAIR_COLS = 147456
MODES = 6
BROADENING = 0.5
BLOCKS = ATOMS // 8
ROWS = 2 * PAIR_COLS // 128
STRIP = 32
DUO = 2 * ORB
NONE = 64

F32 = jnp.float32
BF16 = jnp.bfloat16


def lanes(table, index):
    return jnp.take_along_axis(table, index, axis=1, mode="promise_in_bounds")


def iota(dim):
    return lax.broadcasted_iota(jnp.int32, (8, 128), dim)


def pair_row(cell, block, orbital, part):
    return pl.multiple_of((((cell * BLOCKS + block) * 4 + orbital) * 3 + part) * 8, 8)


def split_store(value, hi_ref, lo_ref, rows, cols):
    hi = value.astype(BF16)
    hi_ref[rows, cols] = hi
    lo_ref[rows, cols] = (value - hi.astype(F32)).astype(BF16)


def store_left(pair, left, row):
    rows = pl.ds(row, STRIP)
    for t in range(2):
        split_store(pair[t], left[0], left[1], rows, slice(t * ORB, (t + 1) * ORB))


def store_right(pair, right, row):
    upper, lower = pl.ds(row, STRIP), pl.ds(pl.multiple_of(row + ORB, STRIP), STRIP)
    real, imag = slice(0, ORB), slice(ORB, DUO)
    split_store(pair[0], right[0], right[1], upper, real)
    split_store(pair[0], right[0], right[1], lower, imag)
    split_store(pair[1], right[0], right[1], upper, imag)
    split_store(-pair[1], right[0], right[1], lower, real)


def product(left, right, out):
    for col in range(0, DUO, 256):
        cols = slice(col, col + 256)
        total = jnp.dot(left[0][...], right[0][:, cols], preferred_element_type=F32)
        total = total + jnp.dot(left[1][...], right[0][:, cols], preferred_element_type=F32)
        total = total + jnp.dot(left[0][...], right[1][:, cols], preferred_element_type=F32)
        out[:, cols] = total


def strips(step):
    def one(index, carry):
        step(pl.multiple_of(index * STRIP, STRIP))
        return carry

    lax.fori_loop(0, ORB // STRIP, one, 0)


def load_pair(ref, row):
    rows = pl.ds(row, STRIP)
    return ref[rows, 0:ORB], ref[rows, ORB:DUO]


def index_tables(shift_ref, block):
    lane = iota(1)
    atom = iota(0) + 8 * block
    col = atom + shift_ref[pl.ds(pl.multiple_of(8 * block, 8), 8), :]
    col = jnp.where(col >= ATOMS, col - ATOMS, col)
    following = jnp.full((8, 128), NONE, jnp.int32)
    first = jnp.full((8, 128), NONE, jnp.int32)
    for n in range(NEIGH - 1, -1, -1):
        here = jnp.broadcast_to(col[:, n : n + 1], (8, 128))
        following = jnp.where((col == here) & (lane < n), n, following)
        first = jnp.where(lane == here, n, first)
    return col, following, first


def unshuffle_in(sigma_ref, cell, block):
    lane = iota(1)
    group = lane // 16
    inner = (lane // 4) % 4
    orbital_j = lane % 4
    natural = [
        sigma_ref[pl.ds(block * 8 * 24 + g * 2 + cell, 8, stride=24), :] for g in range(12)
    ]
    out = []
    for i in range(4):
        for u in range(3):
            if u < 2:
                index = inner * 32 + 16 * u + 4 * i + orbital_j
                sources = range(8)
                pick = group
            else:
                index = inner * 32 + 16 * (lane // 64) + 4 * i + orbital_j
                sources = range(8, 12)
                pick = group % 4 + 8
            value = lanes(natural[sources[0]], index)
            for g in sources[1:]:
                value = jnp.where(pick == g, lanes(natural[g], index), value)
            out.append(value)
    return out


def place_block(shift_ref, sigma_ref, system, pair_ref, chain_ref, table_ref, block):
    lane = iota(1)
    quarter = lane // 4
    orbital_j = lane % 4
    late = 32 + (lane % 64) // 4
    half = lane // 64
    col, following, first = index_tables(shift_ref, block)
    rows8 = pl.ds(pl.multiple_of(8 * block, 8), 8)
    table_ref[0, rows8, :] = lanes(col, quarter)
    table_ref[1, rows8, :] = lanes(col, late)
    for cell in range(2):
        for slot, value in enumerate(unshuffle_in(sigma_ref, cell, block)):
            pair_ref[cell * 12 + slot] = value
    chain_ref[...] = following

    def more(least):
        return least < NEIGH

    def join(least):
        chain = chain_ref[...]
        early_next = lanes(chain, quarter)
        late_next = lanes(chain, late)
        low = (4 * early_next + orbital_j) % 128
        high = (4 * early_next + orbital_j) % 64
        last = 64 * half + (4 * late_next + orbital_j) % 64
        for base in range(0, 24, 3):
            tail = pair_ref[base + 2]
            for t in range(2):
                value = pair_ref[base + t]
                added = jnp.where(
                    early_next < 32,
                    lanes(value, low),
                    jnp.where(early_next < NEIGH, lanes(tail, high + 64 * t), 0.0),
                )
                pair_ref[base + t] = value + added
            pair_ref[base + 2] = tail + jnp.where(late_next < NEIGH, lanes(tail, last), 0.0)
        chain = lanes(chain, chain)
        chain_ref[...] = chain
        return jnp.min(chain)

    lax.while_loop(more, join, jnp.min(following))
    for v in range(3):
        entry = lanes(first, 32 * v + quarter)
        low = (4 * entry + orbital_j) % 128
        high = (4 * entry + orbital_j) % 64
        for cell in range(2):
            for i in range(4):
                base = cell * 12 + i * 3
                rows = pl.ds(32 * block + i, 8, stride=4)
                tail = pair_ref[base + 2]
                for t in range(2):
                    value = jnp.where(
                        entry < 32,
                        lanes(pair_ref[base + t], low),
                        jnp.where(entry < NEIGH, lanes(tail, high + 64 * t), 0.0),
                    )
                    system[cell][3 * t + v, rows, :] -= value


def pick_block(green, table_ref, out_ref, cell, block):
    lane = iota(1)
    orbital_j = lane % 4
    rows8 = pl.ds(pl.multiple_of(8 * block, 8), 8)
    early = table_ref[0, rows8, :]
    late = table_ref[1, rows8, :]
    for i in range(4):
        rows = pl.ds(32 * block + i, 8, stride=4)
        source = [green[s, rows, :] for s in range(6)]
        for u in range(3):
            col = early if u < 2 else late
            index = (4 * col + orbital_j) % 128
            chosen = col // 32
            options = source[3 * u : 3 * u + 3] if u < 2 else source
            if u == 2:
                chosen = chosen + 3 * (lane // 64)
            value = lanes(options[0], index)
            for s in range(1, len(options)):
                value = jnp.where(chosen == s, lanes(options[s], index), value)
            out_ref[pl.ds(pair_row(cell, block, i, u), 8), :] = value


def block_loop(step):
    def one(block, carry):
        step(block)
        return carry

    lax.fori_loop(0, BLOCKS, one, 0)


def load_tiles(ref, row):
    rows = pl.ds(row, STRIP)
    return tuple(
        jnp.concatenate([ref[3 * t + v, rows, :] for v in range(3)], axis=1) for t in range(2)
    )


def store_tiles(pair, ref, row):
    rows = pl.ds(row, STRIP)
    for t in range(2):
        for v in range(3):
            ref[3 * t + v, rows, :] = pair[t][:, 128 * v : 128 * (v + 1)]


def diagonal_mask(row):
    at = lax.broadcasted_iota(jnp.int32, (STRIP, ORB), 0) + row
    return at == lax.broadcasted_iota(jnp.int32, (STRIP, ORB), 1)


def inverse_into(shift, onsite_row, system, fold, diag_ref, col_ref, temp, green, left, right, square):
    diag_ref[...] = jnp.zeros_like(diag_ref)

    def full(row):
        real, imag = load_tiles(system, row)
        mask = diagonal_mask(row)
        real = real + jnp.where(mask, shift - onsite_row, 0.0)
        imag = imag + jnp.where(mask, BROADENING, 0.0)
        if fold is not None:
            fold_real, fold_imag = load_pair(fold, row)
            real, imag = real - fold_real, imag - fold_imag
        return real, imag, mask

    def diagonal(row):
        real, imag, mask = full(row)
        real, imag = jnp.where(mask, real, 0.0), jnp.where(mask, imag, 0.0)
        diag_ref[0:1, :] += jnp.sum(real, axis=0, keepdims=True)
        diag_ref[1:2, :] += jnp.sum(imag, axis=0, keepdims=True)
        down_real = jnp.sum(real, axis=1, keepdims=True)
        down_imag = jnp.sum(imag, axis=1, keepdims=True)
        scale = 1.0 / (down_real * down_real + down_imag * down_imag)
        rows = pl.ds(row, STRIP)
        col_ref[0, rows, :] = jnp.broadcast_to(down_real * scale, (STRIP, 128))
        col_ref[1, rows, :] = jnp.broadcast_to(-down_imag * scale, (STRIP, 128))

    strips(diagonal)
    diag_real, diag_imag = diag_ref[0:1, :], diag_ref[1:2, :]
    scale = 1.0 / (diag_real * diag_real + diag_imag * diag_imag)
    inverse_real, inverse_imag = diag_real * scale, -diag_imag * scale

    def scaled(row):
        real, imag, mask = full(row)
        real, imag = jnp.where(mask, 0.0, real), jnp.where(mask, 0.0, imag)
        pair = (
            real * inverse_real - imag * inverse_imag,
            real * inverse_imag + imag * inverse_real,
        )
        store_tiles(pair, system, row)
        store_left(pair, left, row)
        store_right(pair, right, row)

    strips(scaled)
    product(left, right, square)
    strips(lambda row: store_right(load_pair(square, row), right, row))
    product(left, right, temp)

    def finish(row):
        first_real, first_imag = load_tiles(system, row)
        second_real, second_imag = load_pair(square, row)
        third_real, third_imag = load_pair(temp, row)
        real = jnp.where(diagonal_mask(row), 1.0, 0.0) - first_real + second_real - third_real
        imag = second_imag - first_imag - third_imag
        rows = pl.ds(row, STRIP)
        down_real, down_imag = col_ref[0, rows, 0:1], col_ref[1, rows, 0:1]
        pair = (down_real * real - down_imag * imag, down_real * imag + down_imag * real)
        store_tiles(pair, green, row)
        return pair

    return finish


def green_kernel(
    energy_ref,
    shift_in_ref,
    onsite_ref,
    sigma_ref,
    hop_ref,
    coup_ref,
    out_ref,
    shift_ref,
    table_ref,
    pair_ref,
    chain_ref,
    diag_ref,
    col_ref,
    first_system,
    second_system,
    green,
    temp,
    square,
    *operands,
):
    duos = [(operands[2 * s], operands[2 * s + 1]) for s in range(len(operands) // 2)]
    left_a, left_b, left_v, right_a, right_b, right_v = duos
    shift_ref[...] = jnp.zeros_like(shift_ref)
    shift_ref[:, 0:NEIGH] = shift_in_ref[...]
    system = (first_system, second_system)
    for cell in range(2):
        strips(
            lambda row: store_tiles(
                tuple(-hop_ref[2 * cell + t, pl.ds(row, STRIP), :] for t in range(2)), system[cell], row
            )
        )
    block_loop(
        lambda block: place_block(
            shift_ref, sigma_ref, system, pair_ref, chain_ref, table_ref, block
        )
    )
    strips(lambda row: store_right((coup_ref[0, pl.ds(row, STRIP), :], coup_ref[1, pl.ds(row, STRIP), :]), right_v, row))
    for t in range(2):
        square[:, t * ORB : (t + 1) * ORB] = coup_ref[t].T if t == 0 else -coup_ref[t].T
    strips(lambda row: store_left(load_pair(square, row), left_v, row))
    energy = energy_ref[0]

    finish = inverse_into(
        energy, onsite_ref[0:1, :], first_system, None, diag_ref, col_ref, temp, green, left_a, right_a, square
    )

    def first_done(row):
        pair = finish(row)
        store_left(pair, left_a, row)
        store_right(pair, right_a, row)

    strips(first_done)
    product(left_v, right_a, temp)

    def adjoint_done(row):
        pair = load_pair(temp, row)
        store_left(pair, left_b, row)
        store_right(pair, right_b, row)

    strips(adjoint_done)
    product(left_b, right_v, temp)
    product(left_a, right_v, square)
    strips(lambda row: store_left(load_pair(square, row), left_v, row))
    finish = inverse_into(
        energy, onsite_ref[1:2, :], second_system, temp, diag_ref, col_ref, temp, first_system, left_a, right_a, square
    )
    strips(lambda row: store_right(finish(row), right_a, row))
    block_loop(lambda block: pick_block(first_system, table_ref, out_ref, 1, block))
    product(left_v, right_a, temp)
    strips(lambda row: store_left(load_pair(temp, row), left_b, row))
    product(left_b, right_b, temp)

    def total(row):
        base = load_tiles(green, row)
        added = load_pair(temp, row)
        store_tiles((base[0] + added[0], base[1] + added[1]), green, row)

    strips(total)
    block_loop(lambda block: pick_block(green, table_ref, out_ref, 0, block))


def vmem():
    return pl.BlockSpec(memory_space=pltpu.VMEM)


def smem():
    return pl.BlockSpec(memory_space=pltpu.SMEM)


def green_pairs(energy, neighbor_shift, onsite, sigma_rows, hopping, coupling):
    left = [pltpu.VMEM((ORB, DUO), BF16)] * 2
    right = [pltpu.VMEM((DUO, DUO), BF16)] * 2
    return pl.pallas_call(
        green_kernel,
        out_shape=jax.ShapeDtypeStruct((ROWS, 128), F32),
        in_specs=[smem()] + [vmem()] * 5,
        out_specs=vmem(),
        scratch_shapes=[
            pltpu.VMEM((ATOMS, 128), jnp.int32),
            pltpu.VMEM((2, ATOMS, 128), jnp.int32),
            pltpu.VMEM((24, 8, 128), F32),
            pltpu.VMEM((8, 128), jnp.int32),
            pltpu.VMEM((8, ORB), F32),
            pltpu.VMEM((2, ORB, 128), F32),
            pltpu.VMEM((6, ORB, 128), F32),
            pltpu.VMEM((6, ORB, 128), F32),
            pltpu.VMEM((6, ORB, 128), F32),
            pltpu.VMEM((ORB, DUO), F32),
            pltpu.VMEM((ORB, DUO), F32),
            *left,
            *left,
            *left,
            *right,
            *right,
            *right,
        ],
        compiler_params=pltpu.CompilerParams(vmem_limit_bytes=56 * 2**20),
        name="green_pairs",
    )(energy, neighbor_shift, onsite, sigma_rows, hopping, coupling)


def convolve_kernel(shift_ref, phonon_ref, in_ref, out_ref):
    source_energy = iota(1) // 8
    momentum = iota(1) % 8
    tiles = []
    for m in range(MODES):
        pair = []
        for d in range(2):
            wide = jnp.concatenate([phonon_ref[m, d]] * 16, axis=1)
            pair.append(wide)
        tiles.append(pair)
    rows = []
    for energy in range(16):
        value = jnp.zeros((8, 128), F32)
        for m in range(MODES):
            value = value + jnp.where(source_energy == energy - shift_ref[m], tiles[m][0], 0.0)
            value = value + jnp.where(source_energy == energy + shift_ref[m], tiles[m][1], 0.0)
        rows.append(value)
    kernel = jnp.concatenate(rows, axis=0)
    kernel_hi = kernel.astype(BF16)
    kernel_lo = (kernel - kernel_hi.astype(F32)).astype(BF16)
    for s in range(0, 18, 2):
        value = jnp.concatenate(
            [in_ref[pl.ds(s + k, 128, stride=18), :] for k in range(2)], axis=1
        )
        hi = value.astype(BF16)
        lo = (value - hi.astype(F32)).astype(BF16)
        total = jnp.dot(kernel_hi, hi, preferred_element_type=F32)
        total = total + jnp.dot(kernel_lo, hi, preferred_element_type=F32)
        total = total + jnp.dot(kernel_hi, lo, preferred_element_type=F32)
        for k in range(2):
            out_ref[pl.ds(s + k, 128, stride=18), :] = total[:, 128 * k : 128 * (k + 1)]


def convolve(mode_shift, phonon_kernel, rows):
    return pl.pallas_call(
        convolve_kernel,
        out_shape=jax.ShapeDtypeStruct((ROWS, 128), F32),
        in_specs=[smem(), vmem(), vmem()],
        out_specs=vmem(),
        compiler_params=pltpu.CompilerParams(vmem_limit_bytes=32 * 2**20),
        name="convolve",
    )(mode_shift, phonon_kernel, rows)


def natural_kernel(in_ref, out_ref):
    lane = iota(1)
    orbital_i = (lane // 4) % 4
    part = (lane // 16) % 2
    inner = lane // 32
    orbital_j = lane % 4

    def one(index, carry):
        cell = index // BLOCKS
        block = index % BLOCKS
        source = [
            [in_ref[pl.ds(pair_row(cell, block, i, u), 8), :] for u in range(3)] for i in range(4)
        ]
        for g in range(12):
            if g < 8:
                lane_index = 16 * g + 4 * inner + orbital_j
                options = [(i, t, source[i][t]) for i in range(4) for t in range(2)]
                chosen = 2 * orbital_i + part
            else:
                lane_index = 64 * part + 16 * (g - 8) + 4 * inner + orbital_j
                options = [(i, 0, source[i][2]) for i in range(4)]
                chosen = 2 * orbital_i
            value = lanes(options[0][2], lane_index)
            for i, t, option in options[1:]:
                value = jnp.where(chosen == 2 * i + t, lanes(option, lane_index), value)
            out_ref[pl.ds(block * 8 * 24 + g * 2 + cell, 8, stride=24), :] = value
        return carry

    lax.fori_loop(0, 2 * BLOCKS, one, 0)


def natural(rows):
    return pl.pallas_call(
        natural_kernel,
        out_shape=jax.ShapeDtypeStruct((ROWS, 128), F32),
        in_specs=[vmem()],
        out_specs=vmem(),
        compiler_params=pltpu.CompilerParams(vmem_limit_bytes=32 * 2**20),
        name="natural",
    )(rows)


def rows_of(sigma):
    return sigma.reshape(2, PAIR_COLS // 128, 128).transpose(1, 0, 2).reshape(ROWS, 128)


def exchange(rows):
    parts = rows.reshape(128, 9, 2, 128)
    moved = lax.all_to_all(parts, ("energy", "momentum"), split_axis=0, concat_axis=0, tiled=True)
    return moved.reshape(ROWS, 128)


def body(hopping, coupling, onsite, sigma_in, neighbor_shift, mode_shift, phonon_kernel):
    energies = lax.axis_size("energy")
    energy = 2.0 * (lax.axis_index("energy").astype(F32) + 0.5) / energies
    pairs = green_pairs(
        energy.reshape(1),
        neighbor_shift,
        onsite,
        rows_of(sigma_in),
        hopping.reshape(4, ORB, ORB),
        coupling.reshape(2, ORB, ORB),
    )
    convolved = convolve(mode_shift, phonon_kernel, exchange(pairs))
    result = natural(exchange(convolved))
    result = result.reshape(PAIR_COLS // 128, 2, 128).transpose(1, 0, 2)
    return result.reshape(1, 1, 2, PAIR_COLS)


def solution(mesh):
    return jax.shard_map(
        body,
        mesh=mesh,
        in_specs=(
            P("momentum", None, None, None, None),
            P("momentum", None, None, None),
            P(),
            P("energy", "momentum", None, None),
            P(),
            P(),
            P(),
        ),
        out_specs=P("energy", "momentum", None, None),
        check_vma=False,
    )
```

```python
import jax
import jax.numpy as jnp
from jax import lax
from jax.experimental import pallas as pl
from jax.experimental.pallas import tpu as pltpu
from jax.sharding import PartitionSpec as P

ORB = 384
ATOMS = 96
NEIGH = 48
PAIR_COLS = 147456
MODES = 6
BROADENING = 0.5
BLOCKS = ATOMS // 8
ROWS = 2 * PAIR_COLS // 128
STRIP = 32
DUO = 2 * ORB
TILES = DUO // 128
GROUPS = ATOMS // 4

F32 = jnp.float32
BF16 = jnp.bfloat16


def lanes(table, index):
    return jnp.take_along_axis(table, index, axis=1, mode="promise_in_bounds")


def iota(dim):
    return lax.broadcasted_iota(jnp.int32, (8, 128), dim)


def pair_row(cell, block, orbital, part):
    return pl.multiple_of((((cell * BLOCKS + block) * 4 + orbital) * 3 + part) * 8, 8)


def split(value):
    hi = value.astype(BF16)
    return hi, (value - hi.astype(F32)).astype(BF16)


def to_left(left, tile, parts, rows=slice(None)):
    for ref, part in zip(left, parts):
        ref[rows, 128 * tile : 128 * (tile + 1)] = part


def to_right(right, tile, parts, row=0, count=ORB):
    upper, lower = pl.ds(row, count), pl.ds(row + ORB, count)
    same = slice(128 * tile, 128 * (tile + 1))
    other = (tile + 3) % TILES
    across = slice(128 * other, 128 * (other + 1))
    for ref, part in zip(right, parts):
        ref[upper, same] = part
        ref[lower, across] = part if tile < 3 else -part


def product(left, right, emit, side=None):
    for step in range(3):
        cols = slice(256 * step, 256 * (step + 1))
        total = jnp.dot(left[0][...], right[0][:, cols], preferred_element_type=F32)
        total = total + jnp.dot(left[1][...], right[0][:, cols], preferred_element_type=F32)
        total = total + jnp.dot(left[0][...], right[1][:, cols], preferred_element_type=F32)
        if side is not None:
            side(step)
        for half in range(2):
            emit(2 * step + half, total[:, 128 * half : 128 * (half + 1)])


def fill_tables(shift_ref, table_ref):
    wide = jnp.concatenate([shift_ref[...], jnp.zeros((NEIGH, 128 - ATOMS), jnp.int32)], axis=1)
    wide = jnp.concatenate([wide, jnp.zeros((128 - NEIGH, 128), jnp.int32)], axis=0)
    shift = wide.T
    lane = iota(1)
    for block in range(BLOCKS):
        col = shift[8 * block : 8 * (block + 1), :] + iota(0) + 8 * block
        col = jnp.where(col >= ATOMS, col - ATOMS, col)
        table_ref[0, 8 * block : 8 * (block + 1), :] = lanes(col, lane // 4)
        table_ref[1, 8 * block : 8 * (block + 1), :] = lanes(col, 32 + (lane % 64) // 4)


def place_group(shift_ref, sigma_ref, spread_ref, placed, group):
    start = pl.multiple_of(group * 96, 32)
    values = jnp.concatenate([sigma_ref[pl.ds(start, 96), :], jnp.zeros((32, 128), F32)], axis=0).T
    lane = lax.broadcasted_iota(jnp.int32, (NEIGH, 128), 1)
    n = lax.broadcasted_iota(jnp.int32, (NEIGH, 128), 0)
    atom = lax.rem(lane // 24, 4) + 4 * group
    wide = jnp.concatenate([shift_ref[...], jnp.zeros((NEIGH, 128 - ATOMS), jnp.int32)], axis=1)
    shift = jnp.concatenate([lanes(wide[8 * k : 8 * (k + 1)], atom[:8]) for k in range(NEIGH // 8)], axis=0)
    col = shift + atom
    col = jnp.where(col >= ATOMS, col - ATOMS, col).astype(F32)
    column = lax.broadcasted_iota(jnp.int32, (128, 128), 0).astype(F32)
    hot = []
    for inner in range(4):
        chosen = jnp.sum(jnp.where(n == 4 * ((lane % 24) // 2) + inner, col, 0.0), axis=0, keepdims=True)
        chosen = jnp.where(lane[0:1] < 96, chosen, -1.0)
        hot.append(jnp.where(column == chosen, 1.0, 0.0).astype(BF16))
    hot = jnp.concatenate(hot, axis=1)
    lane16 = lax.broadcasted_iota(jnp.int32, (16, 128), 1)
    kept = [
        [jnp.where((lane16 // 24 == a) & (lane16 % 2 == cell), 1.0, 0.0).astype(BF16) for a in range(4)]
        for cell in range(2)
    ]
    rows = []
    for part in split(values):
        for cell in range(2):
            for t in range(2):
                for a in range(4):
                    rows.append(
                        jnp.concatenate(
                            [part[32 * k + 16 * t : 32 * k + 16 * (t + 1)] * kept[cell][a] for k in range(4)], axis=1
                        )
                    )
    spread = lax.dot_general(
        jnp.concatenate(rows, axis=0), hot, (((1,), (1,)), ((), ())), preferred_element_type=F32
    )
    spread_ref[...] = spread[0:256] + spread[256:512]
    for j in range(4):
        parts = split(spread_ref[pl.ds(j, 64, stride=4), :])
        for ref, part in zip(placed, parts):
            for ct in range(4):
                ref[pl.ds(pl.multiple_of(ORB * ct + 16 * group, 16), 16), 128 * j : 128 * (j + 1)] = part[
                    16 * ct : 16 * (ct + 1)
                ]


def assemble(placed, hop_ref, systems):
    at = lax.broadcasted_iota(jnp.int32, (512, ORB), 0)
    to = lax.broadcasted_iota(jnp.int32, (512, ORB), 1)
    order = jnp.where((at % 128 < ATOMS) & (to == 4 * (at % 128) + at // 128), 1.0, 0.0).astype(BF16)
    for cell in range(2):
        for t in range(2):
            rows = slice(ORB * (2 * cell + t), ORB * (2 * cell + t + 1))
            value = jnp.dot(placed[0][rows, :], order, preferred_element_type=F32)
            value = value + jnp.dot(placed[1][rows, :], order, preferred_element_type=F32)
            value = -hop_ref[2 * cell + t] - value
            for v in range(3):
                systems[cell][3 * t + v] = value[:, 128 * v : 128 * (v + 1)]


def pick_block(green, table_ref, out_ref, cell, block):
    lane = iota(1)
    orbital_j = lane % 4
    rows8 = pl.ds(pl.multiple_of(8 * block, 8), 8)
    source = [
        [green[s, pl.ds(32 * block + i, 8, stride=4), :] for s in range(TILES)] for i in range(4)
    ]
    for late in range(2):
        col = table_ref[late, rows8, :]
        index = (4 * col + orbital_j) % 128
        chosen = col // 32
        moved = [[lanes(value, index) for value in source[i]] for i in range(4)]
        for i in range(4):
            picked = []
            for t in range(2):
                first, second, third = moved[i][3 * t : 3 * t + 3]
                picked.append(jnp.where(chosen == 0, first, jnp.where(chosen == 1, second, third)))
            if late:
                value = jnp.where(lane < 64, picked[0], picked[1])
                out_ref[pl.ds(pair_row(cell, block, i, 2), 8), :] = value
            else:
                for t in range(2):
                    out_ref[pl.ds(pair_row(cell, block, i, t), 8), :] = picked[t]


def inverse_diagonal(shift, onsite_ref, cell, system, row_ref, col_ref):
    eye = lax.broadcasted_iota(jnp.int32, (128, 128), 0) == lax.broadcasted_iota(jnp.int32, (128, 128), 1)
    for v in range(3):
        cols = slice(128 * v, 128 * (v + 1))
        real = system[v, cols, :] + (shift - onsite_ref[cell : cell + 1, cols])
        imag = system[3 + v, cols, :] + BROADENING
        real, imag = jnp.where(eye, real, 0.0), jnp.where(eye, imag, 0.0)
        for axis, ref in ((0, row_ref), (1, col_ref)):
            down_real = jnp.sum(real, axis=axis, keepdims=True)
            down_imag = jnp.sum(imag, axis=axis, keepdims=True)
            scale = 1.0 / (down_real * down_real + down_imag * down_imag)
            for t, part in enumerate((down_real * scale, -down_imag * scale)):
                if axis == 0:
                    ref[t : t + 1, cols] = part
                else:
                    ref[t, cols, :] = jnp.broadcast_to(part, (128, 128))


def scale_strip(system, row_ref, col_ref, base, left, right, row):
    rows = pl.ds(row, STRIP)
    down_real, down_imag = col_ref[0, rows, :], col_ref[1, rows, :]
    at = lax.broadcasted_iota(jnp.int32, (STRIP, 128), 0) + row
    for v in range(3):
        on = at == lax.broadcasted_iota(jnp.int32, (STRIP, 128), 1) + 128 * v
        across_real = row_ref[0:1, 128 * v : 128 * (v + 1)]
        across_imag = row_ref[1:2, 128 * v : 128 * (v + 1)]
        real = jnp.where(on, 0.0, system[v, rows, :])
        imag = jnp.where(on, 0.0, system[3 + v, rows, :])
        real, imag = real * across_real - imag * across_imag, real * across_imag + imag * across_real
        to_right(right, v, split(real), row, STRIP)
        to_right(right, 3 + v, split(imag), row, STRIP)
        real, imag = down_real * real - down_imag * imag, down_real * imag + down_imag * real
        to_left(left, v, split(real), rows)
        to_left(left, 3 + v, split(imag), rows)
        base[v, rows, :] = jnp.where(on, down_real, 0.0) - real
        base[3 + v, rows, :] = jnp.where(on, down_imag, 0.0) - imag


def strips(step, unroll=2):
    def one(index, carry):
        step(pl.multiple_of(index * STRIP, STRIP))
        return carry

    lax.fori_loop(0, ORB // STRIP, one, 0, unroll=unroll)


def green_kernel(
    energy_ref,
    shift_ref,
    onsite_ref,
    sigma_ref,
    hop_in_ref,
    coup_in_ref,
    out_ref,
    table_ref,
    spread_ref,
    row_ref,
    col_ref,
    hop_ref,
    coup_ref,
    first_system,
    second_system,
    base,
    green,
    placed_hi,
    placed_lo,
    sems,
    *operands,
):
    duos = [(operands[2 * s], operands[2 * s + 1]) for s in range(len(operands) // 2)]
    left_a, left_b, left_v, left_u, right_a, right_b, right_v = duos
    hop_copy = pltpu.make_async_copy(hop_in_ref, hop_ref, sems.at[0])
    coup_copy = pltpu.make_async_copy(coup_in_ref, coup_ref, sems.at[1])
    hop_copy.start()
    coup_copy.start()
    energy = energy_ref[0]
    placed = (placed_hi, placed_lo)
    fill_tables(shift_ref, table_ref)

    def place(group, carry):
        place_group(shift_ref, sigma_ref, spread_ref, placed, group)
        return carry

    lax.fori_loop(0, GROUPS, place, 0, unroll=2)
    hop_copy.wait()
    assemble(placed, hop_ref, (first_system, second_system))
    coup_copy.wait()
    for t in range(2):
        turned = coup_ref[t].T
        for v in range(3):
            cols = slice(128 * v, 128 * (v + 1))
            to_right(right_v, 3 * t + v, split(coup_ref[t, :, cols]))
            to_left(left_v, 3 * t + v, split(turned[:, cols] if t == 0 else -turned[:, cols]))

    def second_term(tile, value):
        to_left(left_b, tile, split(value))
        base[tile] += value

    def invert(cell, system, emit):
        inverse_diagonal(energy, onsite_ref, cell, system, row_ref, col_ref)
        strips(lambda row: scale_strip(system, row_ref, col_ref, base, left_a, right_a, row))
        product(left_a, right_a, second_term)
        product(left_b, right_a, lambda tile, value: emit(tile, base[tile] - value))

    def first_green(tile, value):
        green[tile] = value
        parts = split(value)
        to_left(left_a, tile, parts)
        to_right(right_b, tile, parts)

    invert(0, first_system, first_green)

    def adjoint(tile, value):
        parts = split(value)
        to_left(left_b, tile, parts)
        to_right(right_a, tile, parts)

    product(left_v, right_b, adjoint)

    def fold(tile, value):
        second_system[tile] -= value

    product(left_b, right_v, fold)
    product(left_a, right_v, lambda tile, value: to_left(left_u, tile, split(value)))
    inverse_diagonal(energy, onsite_ref, 1, second_system, row_ref, col_ref)
    strips(lambda row: scale_strip(second_system, row_ref, col_ref, base, left_a, right_b, row))
    product(left_a, right_b, second_term)

    def second_green(tile, value):
        value = base[tile] - value
        first_system[tile] = value
        to_right(right_v, tile, split(value))

    product(left_b, right_b, second_green)

    def pick_second(step):
        for block in range(4 * step, 4 * step + 4):
            pick_block(first_system, table_ref, out_ref, 1, block)

    product(left_u, right_v, lambda tile, value: to_left(left_b, tile, split(value)), pick_second)

    def through(tile, value):
        green[tile] += value

    product(left_b, right_a, through)

    def pick(block, carry):
        pick_block(green, table_ref, out_ref, 0, block)
        return carry

    lax.fori_loop(0, BLOCKS, pick, 0, unroll=3)


def vmem():
    return pl.BlockSpec(memory_space=pltpu.VMEM)


def smem():
    return pl.BlockSpec(memory_space=pltpu.SMEM)


def green_pairs(energy, neighbor_shift, onsite, sigma_rows, hopping, coupling):
    left = [pltpu.VMEM((ORB, DUO), BF16)] * 2
    right = [pltpu.VMEM((DUO, DUO), BF16)] * 2
    return pl.pallas_call(
        green_kernel,
        out_shape=jax.ShapeDtypeStruct((ROWS, 128), F32),
        in_specs=[smem()] + [vmem()] * 3 + [pl.BlockSpec(memory_space=pl.ANY)] * 2,
        out_specs=vmem(),
        scratch_shapes=[
            pltpu.VMEM((2, ATOMS, 128), jnp.int32),
            pltpu.VMEM((256, 128), F32),
            pltpu.VMEM((8, ORB), F32),
            pltpu.VMEM((2, ORB, 128), F32),
            pltpu.VMEM((4, ORB, ORB), F32),
            pltpu.VMEM((2, ORB, ORB), F32),
            pltpu.VMEM((TILES, ORB, 128), F32),
            pltpu.VMEM((TILES, ORB, 128), F32),
            pltpu.VMEM((TILES, ORB, 128), F32),
            pltpu.VMEM((TILES, ORB, 128), F32),
            pltpu.VMEM((4 * ORB, 512), BF16),
            pltpu.VMEM((4 * ORB, 512), BF16),
            pltpu.SemaphoreType.DMA((2,)),
            *left,
            *left,
            *left,
            *left,
            *right,
            *right,
            *right,
        ],
        compiler_params=pltpu.CompilerParams(vmem_limit_bytes=56 * 2**20),
        name="green_pairs",
    )(energy, neighbor_shift.T, onsite, sigma_rows, hopping, coupling)


def convolve_kernel(shift_ref, phonon_ref, in_ref, out_ref):
    source_energy = iota(1) // 8
    momentum = iota(1) % 8
    tiles = []
    for m in range(MODES):
        pair = []
        for d in range(2):
            wide = jnp.concatenate([phonon_ref[m, d]] * 16, axis=1)
            pair.append(wide)
        tiles.append(pair)
    rows = []
    for energy in range(16):
        value = jnp.zeros((8, 128), F32)
        for m in range(MODES):
            value = value + jnp.where(source_energy == energy - shift_ref[m], tiles[m][0], 0.0)
            value = value + jnp.where(source_energy == energy + shift_ref[m], tiles[m][1], 0.0)
        rows.append(value)
    kernel = jnp.concatenate(rows, axis=0)
    kernel_hi = kernel.astype(BF16)
    kernel_lo = (kernel - kernel_hi.astype(F32)).astype(BF16)
    for s in range(0, 18, 2):
        value = jnp.concatenate(
            [in_ref[pl.ds(s + k, 128, stride=18), :] for k in range(2)], axis=1
        )
        hi = value.astype(BF16)
        lo = (value - hi.astype(F32)).astype(BF16)
        total = jnp.dot(kernel_hi, hi, preferred_element_type=F32)
        total = total + jnp.dot(kernel_lo, hi, preferred_element_type=F32)
        total = total + jnp.dot(kernel_hi, lo, preferred_element_type=F32)
        for k in range(2):
            out_ref[pl.ds(s + k, 128, stride=18), :] = total[:, 128 * k : 128 * (k + 1)]


def convolve(mode_shift, phonon_kernel, rows):
    return pl.pallas_call(
        convolve_kernel,
        out_shape=jax.ShapeDtypeStruct((ROWS, 128), F32),
        in_specs=[smem(), vmem(), vmem()],
        out_specs=vmem(),
        compiler_params=pltpu.CompilerParams(vmem_limit_bytes=32 * 2**20),
        name="convolve",
    )(mode_shift, phonon_kernel, rows)


def natural_kernel(in_ref, out_ref):
    lane = iota(1)
    orbital_i = (lane // 4) % 4
    part = (lane // 16) % 2
    inner = lane // 32
    orbital_j = lane % 4

    def one(index, carry):
        cell = index // BLOCKS
        block = index % BLOCKS
        source = [
            [in_ref[pl.ds(pair_row(cell, block, i, u), 8), :] for u in range(3)] for i in range(4)
        ]
        for g in range(12):
            if g < 8:
                lane_index = 16 * g + 4 * inner + orbital_j
                options = [(i, t, source[i][t]) for i in range(4) for t in range(2)]
                chosen = 2 * orbital_i + part
            else:
                lane_index = 64 * part + 16 * (g - 8) + 4 * inner + orbital_j
                options = [(i, 0, source[i][2]) for i in range(4)]
                chosen = 2 * orbital_i
            value = lanes(options[0][2], lane_index)
            for i, t, option in options[1:]:
                value = jnp.where(chosen == 2 * i + t, lanes(option, lane_index), value)
            out_ref[pl.ds(block * 8 * 24 + g * 2 + cell, 8, stride=24), :] = value
        return carry

    lax.fori_loop(0, 2 * BLOCKS, one, 0, unroll=3)


def natural(rows):
    return pl.pallas_call(
        natural_kernel,
        out_shape=jax.ShapeDtypeStruct((ROWS, 128), F32),
        in_specs=[vmem()],
        out_specs=vmem(),
        compiler_params=pltpu.CompilerParams(vmem_limit_bytes=32 * 2**20),
        name="natural",
    )(rows)


def rows_of(sigma):
    return sigma.reshape(2, PAIR_COLS // 128, 128).transpose(1, 0, 2).reshape(ROWS, 128)


def exchange(rows):
    parts = rows.reshape(128, 9, 2, 128)
    moved = lax.all_to_all(parts, ("energy", "momentum"), split_axis=0, concat_axis=0, tiled=True)
    return moved.reshape(ROWS, 128)


def body(hopping, coupling, onsite, sigma_in, neighbor_shift, mode_shift, phonon_kernel):
    energies = lax.axis_size("energy")
    energy = 2.0 * (lax.axis_index("energy").astype(F32) + 0.5) / energies
    pairs = green_pairs(
        energy.reshape(1),
        neighbor_shift,
        onsite,
        rows_of(sigma_in),
        hopping.reshape(4, ORB, ORB),
        coupling.reshape(2, ORB, ORB),
    )
    convolved = convolve(mode_shift, phonon_kernel, exchange(pairs))
    result = natural(exchange(convolved))
    result = result.reshape(PAIR_COLS // 128, 2, 128).transpose(1, 0, 2)
    return result.reshape(1, 1, 2, PAIR_COLS)


def solution(mesh):
    return jax.shard_map(
        body,
        mesh=mesh,
        in_specs=(
            P("momentum", None, None, None, None),
            P("momentum", None, None, None),
            P(),
            P("energy", "momentum", None, None),
            P(),
            P(),
            P(),
        ),
        out_specs=P("energy", "momentum", None, None),
        check_vma=False,
    )
```

```python
import jax
import jax.numpy as jnp
from jax import lax
from jax.experimental import pallas as pl
from jax.experimental.pallas import tpu as pltpu
from jax.sharding import PartitionSpec as P

ORB = 384
ATOMS = 96
NEIGH = 48
PAIR_COLS = 147456
MODES = 6
BROADENING = 0.5
BLOCKS = ATOMS // 8
ROWS = 2 * PAIR_COLS // 128
STRIP = 32
DUO = 2 * ORB
TILES = DUO // 128
GROUPS = ATOMS // 4

F32 = jnp.float32
BF16 = jnp.bfloat16


def lanes(table, index):
    return jnp.take_along_axis(table, index, axis=1, mode="promise_in_bounds")


def iota(dim):
    return lax.broadcasted_iota(jnp.int32, (8, 128), dim)


def split(value):
    hi = value.astype(BF16)
    return hi, (value - hi.astype(F32)).astype(BF16)


def to_left(left, tile, parts, rows=slice(None)):
    for ref, part in zip(left, parts):
        ref[rows, 128 * tile : 128 * (tile + 1)] = part


def to_right(right, tile, parts, row=0, count=ORB):
    upper, lower = pl.ds(row, count), pl.ds(row + ORB, count)
    same = slice(128 * tile, 128 * (tile + 1))
    other = (tile + 3) % TILES
    across = slice(128 * other, 128 * (other + 1))
    for ref, part in zip(right, parts):
        ref[upper, same] = part
        ref[lower, across] = part if tile < 3 else -part


def product(left, right, emit, side=None, rows=slice(None)):
    for step in range(3):
        cols = slice(256 * step, 256 * (step + 1))
        total = jnp.dot(left[0][rows, :], right[0][:, cols], preferred_element_type=F32)
        total = total + jnp.dot(left[1][rows, :], right[0][:, cols], preferred_element_type=F32)
        total = total + jnp.dot(left[0][rows, :], right[1][:, cols], preferred_element_type=F32)
        if side is not None:
            side(step)
        for half in range(2):
            emit(2 * step + half, total[:, 128 * half : 128 * (half + 1)])


def fill_tables(shift_ref, table_ref):
    wide = jnp.concatenate([shift_ref[...], jnp.zeros((NEIGH, 128 - ATOMS), jnp.int32)], axis=1)
    wide = jnp.concatenate([wide, jnp.zeros((128 - NEIGH, 128), jnp.int32)], axis=0)
    shift = wide.T
    for v in range(3):
        for block in range(BLOCKS):
            rows = slice(8 * block, 8 * (block + 1))
            col = shift[rows, :] + iota(0) + 8 * block
            col = jnp.where(col >= ATOMS, col - ATOMS, col)
            table_ref[v, rows, :] = lanes(col, 16 * v + iota(1) // 8)


def fill_order(order_ref):
    for start in range(0, 512, 64):
        at = lax.broadcasted_iota(jnp.int32, (64, 512), 0) + start
        to = (at % 128) // 8 * 32 + (at // 4) % 2 * 16 + at // 128 * 4 + at % 4
        hot = to == lax.broadcasted_iota(jnp.int32, (64, 512), 1)
        order_ref[start : start + 64, :] = jnp.where(hot, 1.0, 0.0).astype(BF16)


def place_group(shift_ref, sigma_ref, spread_ref, placed, group):
    start = group * 96
    gap = jnp.zeros((16, 128), F32)
    cells = [sigma_ref[pl.ds(start + cell, 48, stride=2), :] for cell in range(2)]
    values = jnp.concatenate([cells[0], gap, cells[1], gap], axis=0).T
    swapped = pltpu.roll(values, 64, 1)
    lane32 = lax.broadcasted_iota(jnp.int32, (32, 128), 1)
    lane = lax.broadcasted_iota(jnp.int32, (NEIGH, 128), 1)
    n = lax.broadcasted_iota(jnp.int32, (NEIGH, 128), 0)
    inner = lane % 64
    atom = lax.rem(inner // 12, 4) + 4 * group
    wide = jnp.concatenate([shift_ref[...], jnp.zeros((NEIGH, 128 - ATOMS), jnp.int32)], axis=1)
    shift = jnp.concatenate([lanes(wide[8 * k : 8 * (k + 1)], atom[:8]) for k in range(NEIGH // 8)], axis=0)
    col = shift + atom
    col = jnp.where(col >= ATOMS, col - ATOMS, col).astype(F32)
    column = lax.broadcasted_iota(jnp.int32, (128, 128), 0).astype(F32)
    hot = []
    for duo in range(2):
        mine = n == 4 * (inner % 12) + 2 * duo + lane // 64
        chosen = jnp.sum(jnp.where(mine, col, 0.0), axis=0, keepdims=True)
        chosen = jnp.where(inner[0:1] < 48, chosen, -1.0)
        hot.append(jnp.where(column == chosen, 1.0, 0.0).astype(BF16))
    hot = jnp.concatenate(hot, axis=1)
    inner16 = lax.broadcasted_iota(jnp.int32, (16, 128), 1) % 64
    kept = [jnp.where(inner16 // 12 == a, 1.0, 0.0).astype(BF16) for a in range(4)]
    parts = []
    for cell in range(2):
        near, far = (values, swapped) if cell == 0 else (swapped, values)
        parts.append(
            [
                split(jnp.where(lane32 < 64, near[64 * duo : 64 * duo + 32], far[64 * duo + 32 : 64 * duo + 64]))
                for duo in range(2)
            ]
        )
    rows = []
    for part in range(2):
        for cell in range(2):
            for t in range(2):
                for a in range(4):
                    rows.append(
                        jnp.concatenate(
                            [parts[cell][duo][part][16 * t : 16 * (t + 1)] * kept[a] for duo in range(2)], axis=1
                        )
                    )
    spread = lax.dot_general(
        jnp.concatenate(rows, axis=0), hot, (((1,), (1,)), ((), ())), preferred_element_type=F32
    )
    spread_ref[...] = spread[0:256] + spread[256:512]
    for j in range(4):
        pieces = split(spread_ref[pl.ds(j, 64, stride=4), :])
        for ref, piece in zip(placed, pieces):
            for ct in range(4):
                ref[pl.ds(pl.multiple_of(ORB * ct + 16 * group, 16), 16), 128 * j : 128 * (j + 1)] = piece[
                    16 * ct : 16 * (ct + 1)
                ]


def assemble(placed, hop_ref, system, cell, t):
    at = lax.broadcasted_iota(jnp.int32, (512, ORB), 0)
    to = lax.broadcasted_iota(jnp.int32, (512, ORB), 1)
    order = jnp.where((at % 128 < ATOMS) & (to == 4 * (at % 128) + at // 128), 1.0, 0.0).astype(BF16)
    rows = slice(ORB * (2 * cell + t), ORB * (2 * cell + t + 1))
    value = jnp.dot(placed[0][rows, :], order, preferred_element_type=F32)
    value = value + jnp.dot(placed[1][rows, :], order, preferred_element_type=F32)
    value = -hop_ref[2 * cell + t] - value
    for v in range(3):
        system[3 * t + v] = value[:, 128 * v : 128 * (v + 1)]


def pick_atoms(green, table_ref, picked, start):
    lane = iota(1)
    orbital_j = lane % 4
    real = (lane // 4) % 2 == 0
    source = [
        [
            [green[s, pl.ds(4 * (start + 8 * half) + i, 8, stride=4), :] for s in range(TILES)]
            for i in range(4)
        ]
        for half in range(2)
    ]
    for v in range(3):
        chosen_values = []
        for half in range(2):
            col = table_ref[v, pl.ds(start + 8 * half, 8), :]
            index = (4 * col + orbital_j) % 128
            tile = col // 32
            moved = [[lanes(value, index) for value in source[half][i]] for i in range(4)]
            chosen_values.append(
                [
                    jnp.where(
                        tile == 0,
                        jnp.where(real, moved[i][0], moved[i][3]),
                        jnp.where(
                            tile == 1,
                            jnp.where(real, moved[i][1], moved[i][4]),
                            jnp.where(real, moved[i][2], moved[i][5]),
                        ),
                    )
                    for i in range(4)
                ]
            )
        rows = pl.ds(ATOMS * v + start, 16)
        for i in range(4):
            value = jnp.concatenate([chosen_values[0][i], chosen_values[1][i]], axis=0)
            for ref, part in zip(picked, split(value)):
                ref[rows, 128 * i : 128 * (i + 1)] = part


def order_pairs(picked, order_ref, out_ref, cell):
    value = jnp.dot(picked[0][...], order_ref[...], preferred_element_type=F32)
    value = value + jnp.dot(picked[1][...], order_ref[...], preferred_element_type=F32)
    for v in range(3):
        for block in range(BLOCKS):
            row = ATOMS * v + 8 * block
            for g in range(4):
                to = (block * 8 * 12 + 4 * v + g) * 2 + cell
                out_ref[pl.ds(to, 8, stride=24), :] = value[row : row + 8, 128 * g : 128 * (g + 1)]


def inverse_diagonal(shift, onsite_ref, cell, system, row_ref, col_ref):
    eye = lax.broadcasted_iota(jnp.int32, (128, 128), 0) == lax.broadcasted_iota(jnp.int32, (128, 128), 1)
    for v in range(3):
        cols = slice(128 * v, 128 * (v + 1))
        real = system[v, cols, :] + (shift - onsite_ref[cell : cell + 1, cols])
        imag = system[3 + v, cols, :] + BROADENING
        real, imag = jnp.where(eye, real, 0.0), jnp.where(eye, imag, 0.0)
        for axis, ref in ((0, row_ref), (1, col_ref)):
            down_real = jnp.sum(real, axis=axis, keepdims=True)
            down_imag = jnp.sum(imag, axis=axis, keepdims=True)
            scale = 1.0 / (down_real * down_real + down_imag * down_imag)
            for t, part in enumerate((down_real * scale, -down_imag * scale)):
                if axis == 0:
                    ref[t : t + 1, cols] = part
                else:
                    ref[t, cols, :] = jnp.broadcast_to(part, (128, 128))


def scale_strip(system, row_ref, col_ref, base, left, right, row):
    rows = pl.ds(row, STRIP)
    down_real, down_imag = col_ref[0, rows, :], col_ref[1, rows, :]
    at = lax.broadcasted_iota(jnp.int32, (STRIP, 128), 0) + row
    for v in range(3):
        on = at == lax.broadcasted_iota(jnp.int32, (STRIP, 128), 1) + 128 * v
        across_real = row_ref[0:1, 128 * v : 128 * (v + 1)]
        across_imag = row_ref[1:2, 128 * v : 128 * (v + 1)]
        real = jnp.where(on, 0.0, system[v, rows, :])
        imag = jnp.where(on, 0.0, system[3 + v, rows, :])
        real, imag = real * across_real - imag * across_imag, real * across_imag + imag * across_real
        to_right(right, v, split(real), row, STRIP)
        to_right(right, 3 + v, split(imag), row, STRIP)
        real, imag = down_real * real - down_imag * imag, down_real * imag + down_imag * real
        to_left(left, v, split(real), rows)
        to_left(left, 3 + v, split(imag), rows)
        base[v, rows, :] = jnp.where(on, down_real, 0.0) - real
        base[3 + v, rows, :] = jnp.where(on, down_imag, 0.0) - imag


def green_kernel(
    energy_ref,
    shift_ref,
    onsite_ref,
    sigma_ref,
    hop_in_ref,
    coup_in_ref,
    out_ref,
    table_ref,
    order_ref,
    spread_ref,
    row_ref,
    col_ref,
    hop_ref,
    coup_ref,
    first_system,
    second_system,
    base,
    green,
    placed_hi,
    placed_lo,
    picked_hi,
    picked_lo,
    more_hi,
    more_lo,
    sems,
    *operands,
):
    duos = [(operands[2 * s], operands[2 * s + 1]) for s in range(len(operands) // 2)]
    left_a, left_b, left_v, left_u, right_a, right_b, right_v = duos
    hop_copy = pltpu.make_async_copy(hop_in_ref, hop_ref, sems.at[0])
    coup_copy = pltpu.make_async_copy(coup_in_ref, coup_ref, sems.at[1])
    hop_copy.start()
    coup_copy.start()
    energy = energy_ref[0]
    placed = (placed_hi, placed_lo)
    first_picked, second_picked = (picked_hi, picked_lo), (more_hi, more_lo)
    fill_tables(shift_ref, table_ref)
    fill_order(order_ref)

    def place(group, carry):
        place_group(shift_ref, sigma_ref, spread_ref, placed, group)
        return carry

    lax.fori_loop(0, GROUPS, place, 0, unroll=2)
    hop_copy.wait()
    coup_copy.wait()
    for t in range(2):
        assemble(placed, hop_ref, first_system, 0, t)
    inverse_diagonal(energy, onsite_ref, 0, first_system, row_ref, col_ref)
    for t in range(2):
        assemble(placed, hop_ref, second_system, 1, t)
        for strip in range(6 * t, 6 * t + 6):
            scale_strip(first_system, row_ref, col_ref, base, left_a, right_a, strip * STRIP)

    def coupling(step):
        if step == 2:
            return
        turned = coup_ref[step].T
        for v in range(3):
            cols = slice(128 * v, 128 * (v + 1))
            to_right(right_v, 3 * step + v, split(coup_ref[step, :, cols]))
            to_left(left_v, 3 * step + v, split(turned[:, cols] if step == 0 else -turned[:, cols]))

    def second_term(tile, value):
        to_left(left_b, tile, split(value))
        base[tile] += value

    def first_green(tile, value):
        value = base[tile] - value
        green[tile] = value
        parts = split(value)
        to_left(left_a, tile, parts)
        to_right(right_b, tile, parts)

    product(left_a, right_a, second_term, coupling)
    product(left_b, right_a, first_green)

    def adjoint(tile, value):
        parts = split(value)
        to_left(left_b, tile, parts)
        to_right(right_a, tile, parts)

    product(left_v, right_b, adjoint)

    def fold(tile, value):
        second_system[tile] -= value

    product(left_b, right_v, fold)
    inverse_diagonal(energy, onsite_ref, 1, second_system, row_ref, col_ref)

    def scale(step):
        for strip in range(4 * step, 4 * step + 4):
            scale_strip(second_system, row_ref, col_ref, base, left_v, right_b, strip * STRIP)

    product(left_a, right_v, lambda tile, value: to_left(left_u, tile, split(value)), scale)
    product(left_v, right_b, second_term)

    def second_green(tile, value):
        value = base[tile] - value
        first_system[tile] = value
        to_right(right_v, tile, split(value))

    product(left_b, right_b, second_green)

    def pick_second(step):
        for half in range(2):
            pick_atoms(first_system, table_ref, second_picked, 32 * step + 16 * half)

    product(left_u, right_v, lambda tile, value: to_left(left_a, tile, split(value)), pick_second)
    for chunk in range(3):
        rows = slice(128 * chunk, 128 * (chunk + 1))

        def through(tile, value, rows=rows):
            green[tile, rows, :] += value

        def beside(step, chunk=chunk):
            if step == 0 and chunk == 0:
                order_pairs(second_picked, order_ref, out_ref, 1)
            if step < 2 and chunk > 0:
                pick_atoms(green, table_ref, first_picked, 32 * (chunk - 1) + 16 * step)

        product(left_a, right_a, through, beside, rows)
    for half in range(2):
        pick_atoms(green, table_ref, first_picked, 64 + 16 * half)
    order_pairs(first_picked, order_ref, out_ref, 0)


def vmem():
    return pl.BlockSpec(memory_space=pltpu.VMEM)


def smem():
    return pl.BlockSpec(memory_space=pltpu.SMEM)


def green_pairs(energy, neighbor_shift, onsite, sigma_rows, hopping, coupling):
    left = [pltpu.VMEM((ORB, DUO), BF16)] * 2
    right = [pltpu.VMEM((DUO, DUO), BF16)] * 2
    return pl.pallas_call(
        green_kernel,
        out_shape=jax.ShapeDtypeStruct((ROWS, 128), F32),
        in_specs=[smem()] + [vmem()] * 3 + [pl.BlockSpec(memory_space=pl.ANY)] * 2,
        out_specs=vmem(),
        scratch_shapes=[
            pltpu.VMEM((3, ATOMS, 128), jnp.int32),
            pltpu.VMEM((512, 512), BF16),
            pltpu.VMEM((256, 128), F32),
            pltpu.VMEM((8, ORB), F32),
            pltpu.VMEM((2, ORB, 128), F32),
            pltpu.VMEM((4, ORB, ORB), F32),
            pltpu.VMEM((2, ORB, ORB), F32),
            pltpu.VMEM((TILES, ORB, 128), F32),
            pltpu.VMEM((TILES, ORB, 128), F32),
            pltpu.VMEM((TILES, ORB, 128), F32),
            pltpu.VMEM((TILES, ORB, 128), F32),
            pltpu.VMEM((4 * ORB, 512), BF16),
            pltpu.VMEM((4 * ORB, 512), BF16),
            *([pltpu.VMEM((3 * ATOMS, 512), BF16)] * 4),
            pltpu.SemaphoreType.DMA((2,)),
            *left,
            *left,
            *left,
            *left,
            *right,
            *right,
            *right,
        ],
        compiler_params=pltpu.CompilerParams(vmem_limit_bytes=56 * 2**20),
        name="green_pairs",
    )(energy, neighbor_shift.T, onsite, sigma_rows, hopping, coupling)


def convolve_kernel(shift_ref, phonon_ref, in_ref, out_ref):
    source_energy = iota(1) // 8
    momentum = iota(1) % 8
    tiles = []
    for m in range(MODES):
        pair = []
        for d in range(2):
            wide = jnp.concatenate([phonon_ref[m, d]] * 16, axis=1)
            pair.append(wide)
        tiles.append(pair)
    rows = []
    for energy in range(16):
        value = jnp.zeros((8, 128), F32)
        for m in range(MODES):
            value = value + jnp.where(source_energy == energy - shift_ref[m], tiles[m][0], 0.0)
            value = value + jnp.where(source_energy == energy + shift_ref[m], tiles[m][1], 0.0)
        rows.append(value)
    kernel = jnp.concatenate(rows, axis=0)
    kernel_hi = kernel.astype(BF16)
    kernel_lo = (kernel - kernel_hi.astype(F32)).astype(BF16)
    for s in range(0, 18, 2):
        value = jnp.concatenate(
            [in_ref[pl.ds(s + k, 128, stride=18), :] for k in range(2)], axis=1
        )
        hi = value.astype(BF16)
        lo = (value - hi.astype(F32)).astype(BF16)
        total = jnp.dot(kernel_hi, hi, preferred_element_type=F32)
        total = total + jnp.dot(kernel_lo, hi, preferred_element_type=F32)
        total = total + jnp.dot(kernel_hi, lo, preferred_element_type=F32)
        for k in range(2):
            out_ref[pl.ds(s + k, 128, stride=18), :] = total[:, 128 * k : 128 * (k + 1)]


def convolve(mode_shift, phonon_kernel, rows):
    return pl.pallas_call(
        convolve_kernel,
        out_shape=jax.ShapeDtypeStruct((ROWS, 128), F32),
        in_specs=[smem(), vmem(), vmem()],
        out_specs=vmem(),
        compiler_params=pltpu.CompilerParams(vmem_limit_bytes=32 * 2**20),
        name="convolve",
    )(mode_shift, phonon_kernel, rows)


def rows_of(sigma):
    return sigma.reshape(2, PAIR_COLS // 128, 128).transpose(1, 0, 2).reshape(ROWS, 128)


def exchange(rows):
    parts = rows.reshape(128, 9, 2, 128)
    moved = lax.all_to_all(parts, ("energy", "momentum"), split_axis=0, concat_axis=0, tiled=True)
    return moved.reshape(ROWS, 128)


def body(hopping, coupling, onsite, sigma_in, neighbor_shift, mode_shift, phonon_kernel):
    energies = lax.axis_size("energy")
    energy = 2.0 * (lax.axis_index("energy").astype(F32) + 0.5) / energies
    pairs = green_pairs(
        energy.reshape(1),
        neighbor_shift,
        onsite,
        rows_of(sigma_in),
        hopping.reshape(4, ORB, ORB),
        coupling.reshape(2, ORB, ORB),
    )
    convolved = convolve(mode_shift, phonon_kernel, exchange(pairs))
    result = exchange(convolved).reshape(PAIR_COLS // 128, 2, 128).transpose(1, 0, 2)
    return result.reshape(1, 1, 2, PAIR_COLS)


def solution(mesh):
    return jax.shard_map(
        body,
        mesh=mesh,
        in_specs=(
            P("momentum", None, None, None, None),
            P("momentum", None, None, None),
            P(),
            P("energy", "momentum", None, None),
            P(),
            P(),
            P(),
        ),
        out_specs=P("energy", "momentum", None, None),
        check_vma=False,
    )
```

```python
import jax
import jax.numpy as jnp
from jax import lax
from jax.experimental import pallas as pl
from jax.experimental.pallas import tpu as pltpu
from jax.sharding import PartitionSpec as P

ORB = 384
ATOMS = 96
NEIGH = 48
PAIR_COLS = 147456
MODES = 6
BROADENING = 0.5
BLOCKS = ATOMS // 8
ROWS = 2 * PAIR_COLS // 128
STRIP = 32
DUO = 2 * ORB
TILES = DUO // 128
TOGETHER = 4
GROUPS = ATOMS // 4

F32 = jnp.float32
BF16 = jnp.bfloat16


def lanes(table, index):
    return jnp.take_along_axis(table, index, axis=1, mode="promise_in_bounds")


def iota(dim):
    return lax.broadcasted_iota(jnp.int32, (8, 128), dim)


def split(value):
    hi = value.astype(BF16)
    return hi, (value - hi.astype(F32)).astype(BF16)


def to_left(left, tile, parts, rows=slice(None)):
    for ref, part in zip(left, parts):
        ref[rows, 128 * tile : 128 * (tile + 1)] = part


def to_right(right, tile, parts, row=0, count=ORB):
    upper, lower = pl.ds(row, count), pl.ds(row + ORB, count)
    same = slice(128 * tile, 128 * (tile + 1))
    other = (tile + 3) % TILES
    across = slice(128 * other, 128 * (other + 1))
    for ref, part in zip(right, parts):
        ref[upper, same] = part
        ref[lower, across] = part if tile < 3 else -part


def product(left, right, emit, side=None, rows=slice(None)):
    for step in range(3):
        cols = slice(256 * step, 256 * (step + 1))
        total = jnp.dot(left[0][rows, :], right[0][:, cols], preferred_element_type=F32)
        total = total + jnp.dot(left[1][rows, :], right[0][:, cols], preferred_element_type=F32)
        total = total + jnp.dot(left[0][rows, :], right[1][:, cols], preferred_element_type=F32)
        if side is not None:
            side(step)
        for half in range(2):
            emit(2 * step + half, total[:, 128 * half : 128 * (half + 1)])


def fill_tables(shift_ref, table_ref):
    wide = jnp.concatenate([shift_ref[...], jnp.zeros((NEIGH, 128 - ATOMS), jnp.int32)], axis=1)
    wide = jnp.concatenate([wide, jnp.zeros((128 - NEIGH, 128), jnp.int32)], axis=0)
    shift = wide.T
    for v in range(3):
        for block in range(BLOCKS):
            rows = slice(8 * block, 8 * (block + 1))
            col = shift[rows, :] + iota(0) + 8 * block
            col = jnp.where(col >= ATOMS, col - ATOMS, col)
            table_ref[v, rows, :] = lanes(col, 16 * v + iota(1) // 8)


def fill_order(order_ref):
    for start in range(0, 512, 64):
        at = lax.broadcasted_iota(jnp.int32, (64, 512), 0) + start
        to = (at % 128) // 8 * 32 + (at // 4) % 2 * 16 + at // 128 * 4 + at % 4
        hot = to == lax.broadcasted_iota(jnp.int32, (64, 512), 1)
        order_ref[start : start + 64, :] = jnp.where(hot, 1.0, 0.0).astype(BF16)


def spread_group(shift_ref, sigma_ref, group):
    start = group * 96
    gap = jnp.zeros((16, 128), F32)
    cells = [sigma_ref[pl.ds(start + cell, 48, stride=2), :] for cell in range(2)]
    values = jnp.concatenate([cells[0], gap, cells[1], gap], axis=0).T
    swapped = pltpu.roll(values, 64, 1)
    lane32 = lax.broadcasted_iota(jnp.int32, (32, 128), 1)
    lane = lax.broadcasted_iota(jnp.int32, (NEIGH, 128), 1)
    n = lax.broadcasted_iota(jnp.int32, (NEIGH, 128), 0)
    inner = lane % 64
    atom = lax.rem(inner // 12, 4) + 4 * group
    wide = jnp.concatenate([shift_ref[...], jnp.zeros((NEIGH, 128 - ATOMS), jnp.int32)], axis=1)
    shift = jnp.concatenate([lanes(wide[8 * k : 8 * (k + 1)], atom[:8]) for k in range(NEIGH // 8)], axis=0)
    col = shift + atom
    col = jnp.where(col >= ATOMS, col - ATOMS, col).astype(F32)
    column = lax.broadcasted_iota(jnp.int32, (128, 128), 0).astype(F32)
    hot = []
    for duo in range(2):
        mine = n == 4 * (inner % 12) + 2 * duo + lane // 64
        chosen = jnp.sum(jnp.where(mine, col, 0.0), axis=0, keepdims=True)
        chosen = jnp.where(inner[0:1] < 48, chosen, -1.0)
        hot.append(jnp.where(column == chosen, 1.0, 0.0).astype(BF16))
    hot = jnp.concatenate(hot, axis=1)
    inner16 = lax.broadcasted_iota(jnp.int32, (16, 128), 1) % 64
    kept = [jnp.where(inner16 // 12 == a, 1.0, 0.0).astype(BF16) for a in range(4)]
    parts = []
    for cell in range(2):
        near, far = (values, swapped) if cell == 0 else (swapped, values)
        parts.append(
            [
                split(jnp.where(lane32 < 64, near[64 * duo : 64 * duo + 32], far[64 * duo + 32 : 64 * duo + 64]))
                for duo in range(2)
            ]
        )
    rows = []
    for part in range(2):
        for cell in range(2):
            for t in range(2):
                for a in range(4):
                    rows.append(
                        jnp.concatenate(
                            [parts[cell][duo][part][16 * t : 16 * (t + 1)] * kept[a] for duo in range(2)], axis=1
                        )
                    )
    spread = lax.dot_general(
        jnp.concatenate(rows, axis=0), hot, (((1,), (1,)), ((), ())), preferred_element_type=F32
    )
    return spread[0:256] + spread[256:512]


def place_groups(shift_ref, sigma_ref, spread_ref, placed, first):
    for k in range(TOGETHER):
        spread_ref[k] = spread_group(shift_ref, sigma_ref, first + k)
    for k in range(TOGETHER):
        for j in range(4):
            pieces = split(spread_ref[k, pl.ds(j, 64, stride=4), :])
            for ref, piece in zip(placed, pieces):
                for ct in range(4):
                    rows = pl.ds(pl.multiple_of(ORB * ct + 16 * (first + k), 16), 16)
                    ref[rows, 128 * j : 128 * (j + 1)] = piece[16 * ct : 16 * (ct + 1)]


def assemble(placed, hop_ref, system, cell, t):
    at = lax.broadcasted_iota(jnp.int32, (512, ORB), 0)
    to = lax.broadcasted_iota(jnp.int32, (512, ORB), 1)
    order = jnp.where((at % 128 < ATOMS) & (to == 4 * (at % 128) + at // 128), 1.0, 0.0).astype(BF16)
    rows = slice(ORB * (2 * cell + t), ORB * (2 * cell + t + 1))
    value = jnp.dot(placed[0][rows, :], order, preferred_element_type=F32)
    value = value + jnp.dot(placed[1][rows, :], order, preferred_element_type=F32)
    value = -hop_ref[2 * cell + t] - value
    for v in range(3):
        system[3 * t + v] = value[:, 128 * v : 128 * (v + 1)]


def pick_atoms(green, table_ref, picked, start):
    lane = iota(1)
    orbital_j = lane % 4
    real = (lane // 4) % 2 == 0
    source = [
        [
            [green[s, pl.ds(4 * (start + 8 * half) + i, 8, stride=4), :] for s in range(TILES)]
            for i in range(4)
        ]
        for half in range(2)
    ]
    for v in range(3):
        chosen_values = []
        for half in range(2):
            col = table_ref[v, pl.ds(start + 8 * half, 8), :]
            index = (4 * col + orbital_j) % 128
            tile = col // 32
            moved = [[lanes(value, index) for value in source[half][i]] for i in range(4)]
            chosen_values.append(
                [
                    jnp.where(
                        tile == 0,
                        jnp.where(real, moved[i][0], moved[i][3]),
                        jnp.where(
                            tile == 1,
                            jnp.where(real, moved[i][1], moved[i][4]),
                            jnp.where(real, moved[i][2], moved[i][5]),
                        ),
                    )
                    for i in range(4)
                ]
            )
        rows = pl.ds(96 * (start // 32) + 32 * v + start % 32, 16)
        for i in range(4):
            value = jnp.concatenate([chosen_values[0][i], chosen_values[1][i]], axis=0)
            for ref, part in zip(picked, split(value)):
                ref[rows, 128 * i : 128 * (i + 1)] = part


def order_pairs(picked, order_ref, out_ref, cell, chunk):
    rows = slice(96 * chunk, 96 * (chunk + 1))
    value = jnp.dot(picked[0][rows, :], order_ref[...], preferred_element_type=F32)
    value = value + jnp.dot(picked[1][rows, :], order_ref[...], preferred_element_type=F32)
    for v in range(3):
        for block in range(4):
            row = 32 * v + 8 * block
            for g in range(4):
                to = ((32 * chunk + 8 * block) * 12 + 4 * v + g) * 2 + cell
                out_ref[pl.ds(to, 8, stride=24), :] = value[row : row + 8, 128 * g : 128 * (g + 1)]


def inverse_diagonal(shift, onsite_ref, cell, system, row_ref, col_ref):
    eye = lax.broadcasted_iota(jnp.int32, (128, 128), 0) == lax.broadcasted_iota(jnp.int32, (128, 128), 1)
    for v in range(3):
        cols = slice(128 * v, 128 * (v + 1))
        real = system[v, cols, :] + (shift - onsite_ref[cell : cell + 1, cols])
        imag = system[3 + v, cols, :] + BROADENING
        real, imag = jnp.where(eye, real, 0.0), jnp.where(eye, imag, 0.0)
        for axis, ref in ((0, row_ref), (1, col_ref)):
            down_real = jnp.sum(real, axis=axis, keepdims=True)
            down_imag = jnp.sum(imag, axis=axis, keepdims=True)
            scale = 1.0 / (down_real * down_real + down_imag * down_imag)
            for t, part in enumerate((down_real * scale, -down_imag * scale)):
                if axis == 0:
                    ref[t : t + 1, cols] = part
                else:
                    ref[t, cols, :] = jnp.broadcast_to(part, (128, 128))


def scale_strip(system, row_ref, col_ref, base, left, right, row):
    rows = pl.ds(row, STRIP)
    down_real, down_imag = col_ref[0, rows, :], col_ref[1, rows, :]
    at = lax.broadcasted_iota(jnp.int32, (STRIP, 128), 0) + row
    for v in range(3):
        on = at == lax.broadcasted_iota(jnp.int32, (STRIP, 128), 1) + 128 * v
        across_real = row_ref[0:1, 128 * v : 128 * (v + 1)]
        across_imag = row_ref[1:2, 128 * v : 128 * (v + 1)]
        real = jnp.where(on, 0.0, system[v, rows, :])
        imag = jnp.where(on, 0.0, system[3 + v, rows, :])
        real, imag = real * across_real - imag * across_imag, real * across_imag + imag * across_real
        to_right(right, v, split(real), row, STRIP)
        to_right(right, 3 + v, split(imag), row, STRIP)
        real, imag = down_real * real - down_imag * imag, down_real * imag + down_imag * real
        to_left(left, v, split(real), rows)
        to_left(left, 3 + v, split(imag), rows)
        base[v, rows, :] = jnp.where(on, down_real, 0.0) - real
        base[3 + v, rows, :] = jnp.where(on, down_imag, 0.0) - imag


def green_kernel(
    energy_ref,
    shift_ref,
    onsite_ref,
    sigma_in_ref,
    hop_in_ref,
    coup_in_ref,
    out_to_ref,
    sigma_ref,
    out_ref,
    table_ref,
    order_ref,
    spread_ref,
    row_ref,
    col_ref,
    hop_ref,
    coup_ref,
    first_system,
    second_system,
    base,
    green,
    placed_hi,
    placed_lo,
    picked_hi,
    picked_lo,
    more_hi,
    more_lo,
    sems,
    *operands,
):
    duos = [(operands[2 * s], operands[2 * s + 1]) for s in range(len(operands) // 2)]
    left_a, left_b, left_v, left_u, right_a, right_b, right_v = duos
    hop_copy = pltpu.make_async_copy(hop_in_ref, hop_ref, sems.at[0])
    coup_copy = pltpu.make_async_copy(coup_in_ref, coup_ref, sems.at[1])
    sigma_copy = pltpu.make_async_copy(sigma_in_ref, sigma_ref, sems.at[2])
    sigma_copy.start()
    hop_copy.start()
    coup_copy.start()
    energy = energy_ref[0]
    placed = (placed_hi, placed_lo)
    first_picked, second_picked = (picked_hi, picked_lo), (more_hi, more_lo)
    fill_tables(shift_ref, table_ref)
    fill_order(order_ref)

    sigma_copy.wait()

    def place(step, carry):
        place_groups(shift_ref, sigma_ref, spread_ref, placed, step * TOGETHER)
        return carry

    lax.fori_loop(0, GROUPS // TOGETHER, place, 0)
    hop_copy.wait()
    coup_copy.wait()
    for t in range(2):
        assemble(placed, hop_ref, first_system, 0, t)
    inverse_diagonal(energy, onsite_ref, 0, first_system, row_ref, col_ref)
    for t in range(2):
        assemble(placed, hop_ref, second_system, 1, t)
        for strip in range(6 * t, 6 * t + 6):
            scale_strip(first_system, row_ref, col_ref, base, left_a, right_a, strip * STRIP)

    def coupling(step):
        if step == 2:
            return
        turned = coup_ref[step].T
        for v in range(3):
            cols = slice(128 * v, 128 * (v + 1))
            to_right(right_v, 3 * step + v, split(coup_ref[step, :, cols]))
            to_left(left_v, 3 * step + v, split(turned[:, cols] if step == 0 else -turned[:, cols]))

    def second_term(tile, value):
        to_left(left_b, tile, split(value))
        base[tile] += value

    def first_green(tile, value):
        value = base[tile] - value
        green[tile] = value
        parts = split(value)
        to_left(left_a, tile, parts)
        to_right(right_b, tile, parts)

    product(left_a, right_a, second_term, coupling)
    product(left_b, right_a, first_green)

    def adjoint(tile, value):
        parts = split(value)
        to_left(left_b, tile, parts)
        to_right(right_a, tile, parts)

    product(left_v, right_b, adjoint)

    def fold(tile, value):
        second_system[tile] -= value

    product(left_b, right_v, fold)
    inverse_diagonal(energy, onsite_ref, 1, second_system, row_ref, col_ref)

    def scale(step):
        for strip in range(4 * step, 4 * step + 4):
            scale_strip(second_system, row_ref, col_ref, base, left_v, right_b, strip * STRIP)

    product(left_a, right_v, lambda tile, value: to_left(left_u, tile, split(value)), scale)
    product(left_v, right_b, second_term)

    def second_green(tile, value):
        value = base[tile] - value
        first_system[tile] = value
        to_right(right_v, tile, split(value))

    product(left_b, right_b, second_green)

    def pick_second(step):
        for half in range(2):
            pick_atoms(first_system, table_ref, second_picked, 32 * step + 16 * half)

    product(left_u, right_v, lambda tile, value: to_left(left_a, tile, split(value)), pick_second)
    def send(chunk):
        rows = slice(768 * chunk, 768 * (chunk + 1))
        return pltpu.make_async_copy(out_ref.at[rows], out_to_ref.at[rows], sems.at[3 + chunk])

    for chunk in range(3):
        rows = slice(128 * chunk, 128 * (chunk + 1))

        def through(tile, value, rows=rows):
            green[tile, rows, :] += value

        def beside(step, chunk=chunk):
            if step == 0:
                order_pairs(second_picked, order_ref, out_ref, 1, chunk)
            if chunk > 0:
                if step < 2:
                    pick_atoms(green, table_ref, first_picked, 32 * (chunk - 1) + 16 * step)
                else:
                    order_pairs(first_picked, order_ref, out_ref, 0, chunk - 1)

        product(left_a, right_a, through, beside, rows)
        if chunk > 0:
            send(chunk - 1).start()
    for half in range(2):
        pick_atoms(green, table_ref, first_picked, 64 + 16 * half)
    order_pairs(first_picked, order_ref, out_ref, 0, 2)
    send(2).start()
    for chunk in range(3):
        send(chunk).wait()


def vmem():
    return pl.BlockSpec(memory_space=pltpu.VMEM)


def smem():
    return pl.BlockSpec(memory_space=pltpu.SMEM)


def green_pairs(energy, neighbor_shift, onsite, sigma_rows, hopping, coupling):
    left = [pltpu.VMEM((ORB, DUO), BF16)] * 2
    right = [pltpu.VMEM((DUO, DUO), BF16)] * 2
    return pl.pallas_call(
        green_kernel,
        out_shape=jax.ShapeDtypeStruct((ROWS, 128), F32),
        in_specs=[smem()] + [vmem()] * 2 + [pl.BlockSpec(memory_space=pl.ANY)] * 3,
        out_specs=pl.BlockSpec(memory_space=pl.ANY),
        scratch_shapes=[
            pltpu.VMEM((ROWS, 128), F32),
            pltpu.VMEM((ROWS, 128), F32),
            pltpu.VMEM((3, ATOMS, 128), jnp.int32),
            pltpu.VMEM((512, 512), BF16),
            pltpu.VMEM((TOGETHER, 256, 128), F32),
            pltpu.VMEM((8, ORB), F32),
            pltpu.VMEM((2, ORB, 128), F32),
            pltpu.VMEM((4, ORB, ORB), F32),
            pltpu.VMEM((2, ORB, ORB), F32),
            pltpu.VMEM((TILES, ORB, 128), F32),
            pltpu.VMEM((TILES, ORB, 128), F32),
            pltpu.VMEM((TILES, ORB, 128), F32),
            pltpu.VMEM((TILES, ORB, 128), F32),
            pltpu.VMEM((4 * ORB, 512), BF16),
            pltpu.VMEM((4 * ORB, 512), BF16),
            *([pltpu.VMEM((3 * ATOMS, 512), BF16)] * 4),
            pltpu.SemaphoreType.DMA((6,)),
            *left,
            *left,
            *left,
            *left,
            *right,
            *right,
            *right,
        ],
        compiler_params=pltpu.CompilerParams(vmem_limit_bytes=56 * 2**20),
        name="green_pairs",
    )(energy, neighbor_shift.T, onsite, sigma_rows, hopping, coupling)


def convolve_kernel(shift_ref, phonon_ref, in_ref, out_ref):
    source_energy = iota(1) // 8
    momentum = iota(1) % 8
    tiles = []
    for m in range(MODES):
        pair = []
        for d in range(2):
            wide = jnp.concatenate([phonon_ref[m, d]] * 16, axis=1)
            pair.append(wide)
        tiles.append(pair)
    rows = []
    for energy in range(16):
        value = jnp.zeros((8, 128), F32)
        for m in range(MODES):
            value = value + jnp.where(source_energy == energy - shift_ref[m], tiles[m][0], 0.0)
            value = value + jnp.where(source_energy == energy + shift_ref[m], tiles[m][1], 0.0)
        rows.append(value)
    kernel = jnp.concatenate(rows, axis=0)
    kernel_hi = kernel.astype(BF16)
    kernel_lo = (kernel - kernel_hi.astype(F32)).astype(BF16)
    for s in range(0, 18, 2):
        value = jnp.concatenate(
            [in_ref[pl.ds(s + k, 128, stride=18), :] for k in range(2)], axis=1
        )
        hi = value.astype(BF16)
        lo = (value - hi.astype(F32)).astype(BF16)
        total = jnp.dot(kernel_hi, hi, preferred_element_type=F32)
        total = total + jnp.dot(kernel_lo, hi, preferred_element_type=F32)
        total = total + jnp.dot(kernel_hi, lo, preferred_element_type=F32)
        for k in range(2):
            out_ref[pl.ds(s + k, 128, stride=18), :] = total[:, 128 * k : 128 * (k + 1)]


def convolve(mode_shift, phonon_kernel, rows):
    return pl.pallas_call(
        convolve_kernel,
        out_shape=jax.ShapeDtypeStruct((ROWS, 128), F32),
        in_specs=[smem(), vmem(), vmem()],
        out_specs=vmem(),
        compiler_params=pltpu.CompilerParams(vmem_limit_bytes=32 * 2**20),
        name="convolve",
    )(mode_shift, phonon_kernel, rows)


def rows_of(sigma):
    return sigma.reshape(2, PAIR_COLS // 128, 128).transpose(1, 0, 2).reshape(ROWS, 128)


def exchange(parts):
    return lax.all_to_all(parts, ("energy", "momentum"), split_axis=0, concat_axis=0, tiled=True)


def to_parts(rows):
    return rows.reshape(128, 9, 2, 128)


def body(hopping, coupling, onsite, sigma_in, neighbor_shift, mode_shift, phonon_kernel):
    energies = lax.axis_size("energy")
    energy = 2.0 * (lax.axis_index("energy").astype(F32) + 0.5) / energies
    pairs = green_pairs(
        energy.reshape(1),
        neighbor_shift,
        onsite,
        rows_of(sigma_in),
        hopping.reshape(4, ORB, ORB),
        coupling.reshape(2, ORB, ORB),
    )
    convolved = convolve(mode_shift, phonon_kernel, exchange(to_parts(pairs)).reshape(ROWS, 128))
    parts = convolved.reshape(128, 9, 2, 128).transpose(2, 0, 1, 3)
    moved = lax.all_to_all(parts, ("energy", "momentum"), split_axis=1, concat_axis=1, tiled=True)
    return moved.reshape(1, 1, 2, PAIR_COLS)


def solution(mesh):
    return jax.shard_map(
        body,
        mesh=mesh,
        in_specs=(
            P("momentum", None, None, None, None),
            P("momentum", None, None, None),
            P(),
            P("energy", "momentum", None, None),
            P(),
            P(),
            P(),
        ),
        out_specs=P("energy", "momentum", None, None),
        check_vma=False,
    )
```

```python
import jax
import jax.numpy as jnp
from jax import lax
from jax.experimental import pallas as pl
from jax.experimental.pallas import tpu as pltpu
from jax.sharding import PartitionSpec as P

ORB = 384
ATOMS = 96
NEIGH = 48
PAIR_COLS = 147456
MODES = 6
BROADENING = 0.5
BLOCKS = ATOMS // 8
ROWS = 2 * PAIR_COLS // 128
STRIP = 32
DUO = 2 * ORB
TILES = DUO // 128
TOGETHER = 8
GROUPS = ATOMS // 4

F32 = jnp.float32
BF16 = jnp.bfloat16


def lanes(table, index):
    return jnp.take_along_axis(table, index, axis=1, mode="promise_in_bounds")


def iota(dim):
    return lax.broadcasted_iota(jnp.int32, (8, 128), dim)


def split(value):
    hi = value.astype(BF16)
    return hi, (value - hi.astype(F32)).astype(BF16)


def to_left(left, tile, parts, rows=slice(None)):
    for ref, part in zip(left, parts):
        ref[rows, 128 * tile : 128 * (tile + 1)] = part


def to_right(right, tile, parts, row=0, count=ORB):
    upper, lower = pl.ds(row, count), pl.ds(row + ORB, count)
    same = slice(128 * tile, 128 * (tile + 1))
    other = (tile + 3) % TILES
    across = slice(128 * other, 128 * (other + 1))
    for ref, part in zip(right, parts):
        ref[upper, same] = part
        ref[lower, across] = part if tile < 3 else -part


def product(left, right, emit, side=None, rows=slice(None)):
    for step in range(3):
        cols = slice(256 * step, 256 * (step + 1))
        total = jnp.dot(left[0][rows, :], right[0][:, cols], preferred_element_type=F32)
        total = total + jnp.dot(left[1][rows, :], right[0][:, cols], preferred_element_type=F32)
        total = total + jnp.dot(left[0][rows, :], right[1][:, cols], preferred_element_type=F32)
        if side is not None:
            side(step)
        for half in range(2):
            emit(2 * step + half, total[:, 128 * half : 128 * (half + 1)])


def fill_tables(shift_ref, table_ref):
    wide = jnp.concatenate([shift_ref[...], jnp.zeros((NEIGH, 128 - ATOMS), jnp.int32)], axis=1)
    wide = jnp.concatenate([wide, jnp.zeros((128 - NEIGH, 128), jnp.int32)], axis=0)
    shift = wide.T
    for v in range(3):
        for block in range(BLOCKS):
            rows = slice(8 * block, 8 * (block + 1))
            col = shift[rows, :] + iota(0) + 8 * block
            col = jnp.where(col >= ATOMS, col - ATOMS, col)
            table_ref[v, rows, :] = lanes(col, 16 * v + iota(1) // 8)


def fill_order(order_ref):
    for start in range(0, 512, 64):
        at = lax.broadcasted_iota(jnp.int32, (64, 512), 0) + start
        to = (at % 128) // 8 * 32 + (at // 4) % 2 * 16 + at // 128 * 4 + at % 4
        hot = to == lax.broadcasted_iota(jnp.int32, (64, 512), 1)
        order_ref[start : start + 64, :] = jnp.where(hot, 1.0, 0.0).astype(BF16)


def spread_group(shift_ref, sigma_ref, group):
    start = group * 96
    gap = jnp.zeros((16, 128), F32)
    cells = [sigma_ref[pl.ds(start + cell, 48, stride=2), :] for cell in range(2)]
    values = jnp.concatenate([cells[0], gap, cells[1], gap], axis=0).T
    swapped = pltpu.roll(values, 64, 1)
    lane32 = lax.broadcasted_iota(jnp.int32, (32, 128), 1)
    lane = lax.broadcasted_iota(jnp.int32, (NEIGH, 128), 1)
    n = lax.broadcasted_iota(jnp.int32, (NEIGH, 128), 0)
    inner = lane % 64
    atom = lax.rem(inner // 12, 4) + 4 * group
    wide = jnp.concatenate([shift_ref[...], jnp.zeros((NEIGH, 128 - ATOMS), jnp.int32)], axis=1)
    shift = jnp.concatenate([lanes(wide[8 * k : 8 * (k + 1)], atom[:8]) for k in range(NEIGH // 8)], axis=0)
    col = shift + atom
    col = jnp.where(col >= ATOMS, col - ATOMS, col).astype(F32)
    column = lax.broadcasted_iota(jnp.int32, (128, 128), 0).astype(F32)
    hot = []
    for duo in range(2):
        mine = n == 4 * (inner % 12) + 2 * duo + lane // 64
        chosen = jnp.sum(jnp.where(mine, col, 0.0), axis=0, keepdims=True)
        chosen = jnp.where(inner[0:1] < 48, chosen, -1.0)
        hot.append(jnp.where(column == chosen, 1.0, 0.0).astype(BF16))
    hot = jnp.concatenate(hot, axis=1)
    inner16 = lax.broadcasted_iota(jnp.int32, (16, 128), 1) % 64
    kept = [jnp.where(inner16 // 12 == a, 1.0, 0.0).astype(BF16) for a in range(4)]
    parts = []
    for cell in range(2):
        near, far = (values, swapped) if cell == 0 else (swapped, values)
        parts.append(
            [
                split(jnp.where(lane32 < 64, near[64 * duo : 64 * duo + 32], far[64 * duo + 32 : 64 * duo + 64]))
                for duo in range(2)
            ]
        )
    rows = []
    for part in range(2):
        for cell in range(2):
            for t in range(2):
                for a in range(4):
                    rows.append(
                        jnp.concatenate(
                            [parts[cell][duo][part][16 * t : 16 * (t + 1)] * kept[a] for duo in range(2)], axis=1
                        )
                    )
    spread = lax.dot_general(
        jnp.concatenate(rows, axis=0), hot, (((1,), (1,)), ((), ())), preferred_element_type=F32
    )
    return spread[0:256] + spread[256:512]


def place_groups(shift_ref, sigma_ref, spread_ref, placed, first):
    for k in range(TOGETHER):
        spread_ref[k] = spread_group(shift_ref, sigma_ref, first + k)
    for k in range(TOGETHER):
        for j in range(4):
            pieces = split(spread_ref[k, pl.ds(j, 64, stride=4), :])
            for ref, piece in zip(placed, pieces):
                for ct in range(4):
                    rows = pl.ds(pl.multiple_of(ORB * ct + 16 * (first + k), 16), 16)
                    ref[rows, 128 * j : 128 * (j + 1)] = piece[16 * ct : 16 * (ct + 1)]


def assemble(placed, hop_ref, system, cell, t):
    at = lax.broadcasted_iota(jnp.int32, (512, ORB), 0)
    to = lax.broadcasted_iota(jnp.int32, (512, ORB), 1)
    order = jnp.where((at % 128 < ATOMS) & (to == 4 * (at % 128) + at // 128), 1.0, 0.0).astype(BF16)
    rows = slice(ORB * (2 * cell + t), ORB * (2 * cell + t + 1))
    value = jnp.dot(placed[0][rows, :], order, preferred_element_type=F32)
    value = value + jnp.dot(placed[1][rows, :], order, preferred_element_type=F32)
    value = -hop_ref[2 * cell + t] - value
    for v in range(3):
        system[3 * t + v] = value[:, 128 * v : 128 * (v + 1)]


def pick_atoms(green, table_ref, picked, start):
    lane = iota(1)
    orbital_j = lane % 4
    real = (lane // 4) % 2 == 0
    source = [
        [
            [green[s, pl.ds(4 * (start + 8 * half) + i, 8, stride=4), :] for s in range(TILES)]
            for i in range(4)
        ]
        for half in range(2)
    ]
    for v in range(3):
        chosen_values = []
        for half in range(2):
            col = table_ref[v, pl.ds(start + 8 * half, 8), :]
            index = (4 * col + orbital_j) % 128
            tile = col // 32
            moved = [[lanes(value, index) for value in source[half][i]] for i in range(4)]
            chosen_values.append(
                [
                    jnp.where(
                        tile == 0,
                        jnp.where(real, moved[i][0], moved[i][3]),
                        jnp.where(
                            tile == 1,
                            jnp.where(real, moved[i][1], moved[i][4]),
                            jnp.where(real, moved[i][2], moved[i][5]),
                        ),
                    )
                    for i in range(4)
                ]
            )
        rows = pl.ds(96 * (start // 32) + 32 * v + start % 32, 16)
        for i in range(4):
            value = jnp.concatenate([chosen_values[0][i], chosen_values[1][i]], axis=0)
            for ref, part in zip(picked, split(value)):
                ref[rows, 128 * i : 128 * (i + 1)] = part


def order_pairs(picked, order_ref, out_ref, cell, chunk):
    rows = slice(96 * chunk, 96 * (chunk + 1))
    value = jnp.dot(picked[0][rows, :], order_ref[...], preferred_element_type=F32)
    value = value + jnp.dot(picked[1][rows, :], order_ref[...], preferred_element_type=F32)
    for v in range(3):
        for block in range(4):
            row = 32 * v + 8 * block
            for g in range(4):
                to = ((32 * chunk + 8 * block) * 12 + 4 * v + g) * 2 + cell
                out_ref[pl.ds(to, 8, stride=24), :] = value[row : row + 8, 128 * g : 128 * (g + 1)]


def inverse_diagonal(shift, onsite_ref, cell, system, row_ref, col_ref):
    eye = lax.broadcasted_iota(jnp.int32, (128, 128), 0) == lax.broadcasted_iota(jnp.int32, (128, 128), 1)
    for v in range(3):
        cols = slice(128 * v, 128 * (v + 1))
        real = system[v, cols, :] + (shift - onsite_ref[cell : cell + 1, cols])
        imag = system[3 + v, cols, :] + BROADENING
        real, imag = jnp.where(eye, real, 0.0), jnp.where(eye, imag, 0.0)
        for axis, ref in ((0, row_ref), (1, col_ref)):
            down_real = jnp.sum(real, axis=axis, keepdims=True)
            down_imag = jnp.sum(imag, axis=axis, keepdims=True)
            scale = 1.0 / (down_real * down_real + down_imag * down_imag)
            for t, part in enumerate((down_real * scale, -down_imag * scale)):
                if axis == 0:
                    ref[t : t + 1, cols] = part
                else:
                    ref[t, cols, :] = jnp.broadcast_to(part, (128, 128))


def scale_strip(system, row_ref, col_ref, base, left, right, row):
    rows = pl.ds(row, STRIP)
    down_real, down_imag = col_ref[0, rows, :], col_ref[1, rows, :]
    at = lax.broadcasted_iota(jnp.int32, (STRIP, 128), 0) + row
    for v in range(3):
        on = at == lax.broadcasted_iota(jnp.int32, (STRIP, 128), 1) + 128 * v
        across_real = row_ref[0:1, 128 * v : 128 * (v + 1)]
        across_imag = row_ref[1:2, 128 * v : 128 * (v + 1)]
        real = jnp.where(on, 0.0, system[v, rows, :])
        imag = jnp.where(on, 0.0, system[3 + v, rows, :])
        real, imag = real * across_real - imag * across_imag, real * across_imag + imag * across_real
        to_right(right, v, split(real), row, STRIP)
        to_right(right, 3 + v, split(imag), row, STRIP)
        real, imag = down_real * real - down_imag * imag, down_real * imag + down_imag * real
        to_left(left, v, split(real), rows)
        to_left(left, 3 + v, split(imag), rows)
        base[v, rows, :] = jnp.where(on, down_real, 0.0) - real
        base[3 + v, rows, :] = jnp.where(on, down_imag, 0.0) - imag


def green_kernel(
    energy_ref,
    shift_ref,
    onsite_ref,
    sigma_in_ref,
    hop_in_ref,
    coup_in_ref,
    out_to_ref,
    sigma_ref,
    out_ref,
    table_ref,
    order_ref,
    spread_ref,
    row_ref,
    col_ref,
    hop_ref,
    coup_ref,
    first_system,
    second_system,
    base,
    green,
    placed_hi,
    placed_lo,
    picked_hi,
    picked_lo,
    more_hi,
    more_lo,
    sems,
    *operands,
):
    duos = [(operands[2 * s], operands[2 * s + 1]) for s in range(len(operands) // 2)]
    left_a, left_b, left_v, left_u, right_a, right_b, right_v = duos
    hop_copy = pltpu.make_async_copy(hop_in_ref, hop_ref, sems.at[0])
    coup_copy = pltpu.make_async_copy(coup_in_ref, coup_ref, sems.at[1])
    sigma_copy = pltpu.make_async_copy(sigma_in_ref, sigma_ref, sems.at[2])
    sigma_copy.start()
    hop_copy.start()
    coup_copy.start()
    energy = energy_ref[0]
    placed = (placed_hi, placed_lo)
    first_picked, second_picked = (picked_hi, picked_lo), (more_hi, more_lo)
    fill_tables(shift_ref, table_ref)
    fill_order(order_ref)

    sigma_copy.wait()

    def place(step, carry):
        place_groups(shift_ref, sigma_ref, spread_ref, placed, step * TOGETHER)
        return carry

    lax.fori_loop(0, GROUPS // TOGETHER, place, 0)
    hop_copy.wait()
    coup_copy.wait()
    for t in range(2):
        assemble(placed, hop_ref, first_system, 0, t)
    inverse_diagonal(energy, onsite_ref, 0, first_system, row_ref, col_ref)
    for t in range(2):
        assemble(placed, hop_ref, second_system, 1, t)
        for strip in range(6 * t, 6 * t + 6):
            scale_strip(first_system, row_ref, col_ref, base, left_a, right_a, strip * STRIP)

    def coupling(step):
        if step == 2:
            return
        turned = coup_ref[step].T
        for v in range(3):
            cols = slice(128 * v, 128 * (v + 1))
            to_right(right_v, 3 * step + v, split(coup_ref[step, :, cols]))
            to_left(left_v, 3 * step + v, split(turned[:, cols] if step == 0 else -turned[:, cols]))

    def second_term(tile, value):
        to_left(left_b, tile, split(value))
        base[tile] += value

    def first_green(tile, value):
        value = base[tile] - value
        green[tile] = value
        parts = split(value)
        to_left(left_a, tile, parts)
        to_right(right_b, tile, parts)

    product(left_a, right_a, second_term, coupling)
    product(left_b, right_a, first_green)

    def adjoint(tile, value):
        parts = split(value)
        to_left(left_b, tile, parts)
        to_right(right_a, tile, parts)

    product(left_v, right_b, adjoint)

    def fold(tile, value):
        second_system[tile] -= value

    product(left_b, right_v, fold)
    inverse_diagonal(energy, onsite_ref, 1, second_system, row_ref, col_ref)

    def scale(step):
        for strip in range(4 * step, 4 * step + 4):
            scale_strip(second_system, row_ref, col_ref, base, left_v, right_b, strip * STRIP)

    product(left_a, right_v, lambda tile, value: to_left(left_u, tile, split(value)), scale)
    product(left_v, right_b, second_term)

    def second_green(tile, value):
        value = base[tile] - value
        first_system[tile] = value
        to_right(right_v, tile, split(value))

    product(left_b, right_b, second_green)

    def pick_second(step):
        for half in range(2):
            pick_atoms(first_system, table_ref, second_picked, 32 * step + 16 * half)

    product(left_u, right_v, lambda tile, value: to_left(left_a, tile, split(value)), pick_second)
    def send(chunk):
        rows = slice(768 * chunk, 768 * (chunk + 1))
        return pltpu.make_async_copy(out_ref.at[rows], out_to_ref.at[rows], sems.at[3 + chunk])

    for chunk in range(3):
        rows = slice(128 * chunk, 128 * (chunk + 1))

        def through(tile, value, rows=rows):
            green[tile, rows, :] += value

        def beside(step, chunk=chunk):
            if step == 0:
                order_pairs(second_picked, order_ref, out_ref, 1, chunk)
            if chunk > 0:
                if step < 2:
                    pick_atoms(green, table_ref, first_picked, 32 * (chunk - 1) + 16 * step)
                else:
                    order_pairs(first_picked, order_ref, out_ref, 0, chunk - 1)

        product(left_a, right_a, through, beside, rows)
        if chunk > 0:
            send(chunk - 1).start()
    for half in range(2):
        pick_atoms(green, table_ref, first_picked, 64 + 16 * half)
    order_pairs(first_picked, order_ref, out_ref, 0, 2)
    send(2).start()
    for chunk in range(3):
        send(chunk).wait()


def vmem():
    return pl.BlockSpec(memory_space=pltpu.VMEM)


def smem():
    return pl.BlockSpec(memory_space=pltpu.SMEM)


def green_pairs(energy, neighbor_shift, onsite, sigma_rows, hopping, coupling):
    left = [pltpu.VMEM((ORB, DUO), BF16)] * 2
    right = [pltpu.VMEM((DUO, DUO), BF16)] * 2
    return pl.pallas_call(
        green_kernel,
        out_shape=jax.ShapeDtypeStruct((ROWS, 128), F32),
        in_specs=[smem()] + [vmem()] * 2 + [pl.BlockSpec(memory_space=pl.ANY)] * 3,
        out_specs=pl.BlockSpec(memory_space=pl.ANY),
        scratch_shapes=[
            pltpu.VMEM((ROWS, 128), F32),
            pltpu.VMEM((ROWS, 128), F32),
            pltpu.VMEM((3, ATOMS, 128), jnp.int32),
            pltpu.VMEM((512, 512), BF16),
            pltpu.VMEM((TOGETHER, 256, 128), F32),
            pltpu.VMEM((8, ORB), F32),
            pltpu.VMEM((2, ORB, 128), F32),
            pltpu.VMEM((4, ORB, ORB), F32),
            pltpu.VMEM((2, ORB, ORB), F32),
            pltpu.VMEM((TILES, ORB, 128), F32),
            pltpu.VMEM((TILES, ORB, 128), F32),
            pltpu.VMEM((TILES, ORB, 128), F32),
            pltpu.VMEM((TILES, ORB, 128), F32),
            pltpu.VMEM((4 * ORB, 512), BF16),
            pltpu.VMEM((4 * ORB, 512), BF16),
            *([pltpu.VMEM((3 * ATOMS, 512), BF16)] * 4),
            pltpu.SemaphoreType.DMA((6,)),
            *left,
            *left,
            *left,
            *left,
            *right,
            *right,
            *right,
        ],
        compiler_params=pltpu.CompilerParams(vmem_limit_bytes=56 * 2**20),
        name="green_pairs",
    )(energy, neighbor_shift.T, onsite, sigma_rows, hopping, coupling)


def convolve_kernel(shift_ref, phonon_ref, in_ref, out_ref):
    source_energy = iota(1) // 8
    momentum = iota(1) % 8
    tiles = []
    for m in range(MODES):
        pair = []
        for d in range(2):
            wide = jnp.concatenate([phonon_ref[m, d]] * 16, axis=1)
            pair.append(wide)
        tiles.append(pair)
    rows = []
    for energy in range(16):
        value = jnp.zeros((8, 128), F32)
        for m in range(MODES):
            value = value + jnp.where(source_energy == energy - shift_ref[m], tiles[m][0], 0.0)
            value = value + jnp.where(source_energy == energy + shift_ref[m], tiles[m][1], 0.0)
        rows.append(value)
    kernel = jnp.concatenate(rows, axis=0)
    kernel_hi = kernel.astype(BF16)
    kernel_lo = (kernel - kernel_hi.astype(F32)).astype(BF16)
    for s in range(0, 18, 2):
        value = jnp.concatenate(
            [in_ref[pl.ds(s + k, 128, stride=18), :] for k in range(2)], axis=1
        )
        hi = value.astype(BF16)
        lo = (value - hi.astype(F32)).astype(BF16)
        total = jnp.dot(kernel_hi, hi, preferred_element_type=F32)
        total = total + jnp.dot(kernel_lo, hi, preferred_element_type=F32)
        total = total + jnp.dot(kernel_hi, lo, preferred_element_type=F32)
        for k in range(2):
            out_ref[pl.ds(s + k, 128, stride=18), :] = total[:, 128 * k : 128 * (k + 1)]


def convolve(mode_shift, phonon_kernel, rows):
    return pl.pallas_call(
        convolve_kernel,
        out_shape=jax.ShapeDtypeStruct((ROWS, 128), F32),
        in_specs=[smem(), vmem(), vmem()],
        out_specs=vmem(),
        compiler_params=pltpu.CompilerParams(vmem_limit_bytes=32 * 2**20),
        name="convolve",
    )(mode_shift, phonon_kernel, rows)


def rows_of(sigma):
    return sigma.reshape(2, PAIR_COLS // 128, 128).transpose(1, 0, 2).reshape(ROWS, 128)


def exchange(parts):
    return lax.all_to_all(parts, ("energy", "momentum"), split_axis=0, concat_axis=0, tiled=True)


def to_parts(rows):
    return rows.reshape(128, 9, 2, 128)


def body(hopping, coupling, onsite, sigma_in, neighbor_shift, mode_shift, phonon_kernel):
    energies = lax.axis_size("energy")
    energy = 2.0 * (lax.axis_index("energy").astype(F32) + 0.5) / energies
    pairs = green_pairs(
        energy.reshape(1),
        neighbor_shift,
        onsite,
        rows_of(sigma_in),
        hopping.reshape(4, ORB, ORB),
        coupling.reshape(2, ORB, ORB),
    )
    convolved = convolve(mode_shift, phonon_kernel, exchange(to_parts(pairs)).reshape(ROWS, 128))
    parts = convolved.reshape(128, 9, 2, 128).transpose(2, 0, 1, 3)
    moved = lax.all_to_all(parts, ("energy", "momentum"), split_axis=1, concat_axis=1, tiled=True)
    return moved.reshape(1, 1, 2, PAIR_COLS)


def solution(mesh):
    return jax.shard_map(
        body,
        mesh=mesh,
        in_specs=(
            P("momentum", None, None, None, None),
            P("momentum", None, None, None),
            P(),
            P("energy", "momentum", None, None),
            P(),
            P(),
            P(),
        ),
        out_specs=P("energy", "momentum", None, None),
        check_vma=False,
    )
```

```python
import jax
import jax.numpy as jnp
from jax import lax
from jax.experimental import pallas as pl
from jax.experimental.pallas import tpu as pltpu
from jax.sharding import PartitionSpec as P

ORB = 384
ATOMS = 96
NEIGH = 48
PAIR_COLS = 147456
MODES = 6
BROADENING = 0.5
BLOCKS = ATOMS // 8
ROWS = 2 * PAIR_COLS // 128
STRIP = 32
DUO = 2 * ORB
TILES = DUO // 128
TOGETHER = 24
GROUPS = ATOMS // 4

F32 = jnp.float32
BF16 = jnp.bfloat16


def lanes(table, index):
    return jnp.take_along_axis(table, index, axis=1, mode="promise_in_bounds")


def iota(dim):
    return lax.broadcasted_iota(jnp.int32, (8, 128), dim)


def split(value):
    hi = value.astype(BF16)
    return hi, (value - hi.astype(F32)).astype(BF16)


def to_left(left, tile, parts, rows=slice(None)):
    for ref, part in zip(left, parts):
        ref[rows, 128 * tile : 128 * (tile + 1)] = part


def to_right(right, tile, parts, row=0, count=ORB):
    upper, lower = pl.ds(row, count), pl.ds(row + ORB, count)
    same = slice(128 * tile, 128 * (tile + 1))
    other = (tile + 3) % TILES
    across = slice(128 * other, 128 * (other + 1))
    for ref, part in zip(right, parts):
        ref[upper, same] = part
        ref[lower, across] = part if tile < 3 else -part


def product(left, right, emit, side=None, rows=slice(None)):
    for step in range(3):
        cols = slice(256 * step, 256 * (step + 1))
        total = jnp.dot(left[0][rows, :], right[0][:, cols], preferred_element_type=F32)
        total = total + jnp.dot(left[1][rows, :], right[0][:, cols], preferred_element_type=F32)
        total = total + jnp.dot(left[0][rows, :], right[1][:, cols], preferred_element_type=F32)
        if side is not None:
            side(step)
        for half in range(2):
            emit(2 * step + half, total[:, 128 * half : 128 * (half + 1)])


def fill_tables(shift_ref, table_ref):
    wide = jnp.concatenate([shift_ref[...], jnp.zeros((NEIGH, 128 - ATOMS), jnp.int32)], axis=1)
    wide = jnp.concatenate([wide, jnp.zeros((128 - NEIGH, 128), jnp.int32)], axis=0)
    shift = wide.T
    for v in range(3):
        for block in range(BLOCKS):
            rows = slice(8 * block, 8 * (block + 1))
            col = shift[rows, :] + iota(0) + 8 * block
            col = jnp.where(col >= ATOMS, col - ATOMS, col)
            table_ref[v, rows, :] = lanes(col, 16 * v + iota(1) // 8)


def fill_order(order_ref):
    for start in range(0, 512, 64):
        at = lax.broadcasted_iota(jnp.int32, (64, 512), 0) + start
        to = (at % 128) // 8 * 32 + (at // 4) % 2 * 16 + at // 128 * 4 + at % 4
        hot = to == lax.broadcasted_iota(jnp.int32, (64, 512), 1)
        order_ref[start : start + 64, :] = jnp.where(hot, 1.0, 0.0).astype(BF16)


def fill_hot(shift_ref, hot_ref, group):
    lane = lax.broadcasted_iota(jnp.int32, (NEIGH, 128), 1)
    n = lax.broadcasted_iota(jnp.int32, (NEIGH, 128), 0)
    inner = lane % 64
    atom = lax.rem(inner // 12, 4) + 4 * group
    wide = jnp.concatenate([shift_ref[...], jnp.zeros((NEIGH, 128 - ATOMS), jnp.int32)], axis=1)
    shift = jnp.concatenate([lanes(wide[8 * k : 8 * (k + 1)], atom[:8]) for k in range(NEIGH // 8)], axis=0)
    col = shift + atom
    col = jnp.where(col >= ATOMS, col - ATOMS, col).astype(F32)
    column = lax.broadcasted_iota(jnp.int32, (128, 128), 0).astype(F32)
    for duo in range(2):
        mine = n == 4 * (inner % 12) + 2 * duo + lane // 64
        chosen = jnp.sum(jnp.where(mine, col, 0.0), axis=0, keepdims=True)
        chosen = jnp.where(inner[0:1] < 48, chosen, -1.0)
        hot_ref[group, :, 128 * duo : 128 * (duo + 1)] = jnp.where(column == chosen, 1.0, 0.0).astype(BF16)


def spread_groups(sigma_ref, hot_ref, cell, first):
    gap = jnp.zeros((16, 128), F32)
    groups = [sigma_ref[pl.ds((first + k) * 96 + cell, 48, stride=2), :] for k in range(2)]
    values = jnp.concatenate([groups[0], gap, groups[1], gap], axis=0).T
    swapped = pltpu.roll(values, 64, 1)
    lane32 = lax.broadcasted_iota(jnp.int32, (32, 128), 1)
    inner16 = lax.broadcasted_iota(jnp.int32, (16, 128), 1) % 64
    kept = [jnp.where(inner16 // 12 == a, 1.0, 0.0).astype(BF16) for a in range(4)]
    out = []
    for k in range(2):
        near, far = (values, swapped) if k == 0 else (swapped, values)
        parts = [
            split(jnp.where(lane32 < 64, near[64 * duo : 64 * duo + 32], far[64 * duo + 32 : 64 * duo + 64]))
            for duo in range(2)
        ]
        rows = [
            jnp.concatenate([parts[duo][part][16 * t : 16 * (t + 1)] * kept[a] for duo in range(2)], axis=1)
            for part in range(2)
            for t in range(2)
            for a in range(4)
        ]
        spread = lax.dot_general(
            jnp.concatenate(rows, axis=0), hot_ref[first + k], (((1,), (1,)), ((), ())), preferred_element_type=F32
        )
        out.append(spread[0:128] + spread[128:256])
    return out


def place_groups(sigma_ref, hot_ref, spread_ref, placed, cell, first, count):
    for k in range(0, count, 2):
        for h, value in enumerate(spread_groups(sigma_ref, hot_ref, cell, first + k)):
            spread_ref[k + h] = value
    for k in range(count):
        for j in range(4):
            pieces = split(spread_ref[k, pl.ds(j, 32, stride=4), :])
            for ref, piece in zip(placed, pieces):
                for t in range(2):
                    rows = pl.ds(pl.multiple_of(ORB * (2 * cell + t) + 16 * (first + k), 16), 16)
                    ref[rows, 128 * j : 128 * (j + 1)] = piece[16 * t : 16 * (t + 1)]


def assemble(placed, hop_ref, system, cell, t):
    at = lax.broadcasted_iota(jnp.int32, (512, ORB), 0)
    to = lax.broadcasted_iota(jnp.int32, (512, ORB), 1)
    order = jnp.where((at % 128 < ATOMS) & (to == 4 * (at % 128) + at // 128), 1.0, 0.0).astype(BF16)
    rows = slice(ORB * (2 * cell + t), ORB * (2 * cell + t + 1))
    value = jnp.dot(placed[0][rows, :], order, preferred_element_type=F32)
    value = value + jnp.dot(placed[1][rows, :], order, preferred_element_type=F32)
    value = -hop_ref[2 * cell + t] - value
    for v in range(3):
        system[3 * t + v] = value[:, 128 * v : 128 * (v + 1)]


def pick_atoms(green, table_ref, picked, start):
    lane = iota(1)
    orbital_j = lane % 4
    real = (lane // 4) % 2 == 0
    source = [
        [
            [green[s, pl.ds(4 * (start + 8 * half) + i, 8, stride=4), :] for s in range(TILES)]
            for i in range(4)
        ]
        for half in range(2)
    ]
    for v in range(3):
        chosen_values = []
        for half in range(2):
            col = table_ref[v, pl.ds(start + 8 * half, 8), :]
            index = (4 * col + orbital_j) % 128
            tile = col // 32
            moved = [[lanes(value, index) for value in source[half][i]] for i in range(4)]
            chosen_values.append(
                [
                    jnp.where(
                        tile == 0,
                        jnp.where(real, moved[i][0], moved[i][3]),
                        jnp.where(
                            tile == 1,
                            jnp.where(real, moved[i][1], moved[i][4]),
                            jnp.where(real, moved[i][2], moved[i][5]),
                        ),
                    )
                    for i in range(4)
                ]
            )
        rows = pl.ds(96 * (start // 32) + 32 * v + start % 32, 16)
        for i in range(4):
            value = jnp.concatenate([chosen_values[0][i], chosen_values[1][i]], axis=0)
            for ref, part in zip(picked, split(value)):
                ref[rows, 128 * i : 128 * (i + 1)] = part


def order_pairs(picked, order_ref, out_ref, cell, chunk):
    rows = slice(96 * chunk, 96 * (chunk + 1))
    value = jnp.dot(picked[0][rows, :], order_ref[...], preferred_element_type=F32)
    value = value + jnp.dot(picked[1][rows, :], order_ref[...], preferred_element_type=F32)
    for v in range(3):
        for block in range(4):
            row = 32 * v + 8 * block
            for g in range(4):
                to = ((32 * chunk + 8 * block) * 12 + 4 * v + g) * 2 + cell
                out_ref[pl.ds(to, 8, stride=24), :] = value[row : row + 8, 128 * g : 128 * (g + 1)]


def inverse_diagonal(shift, onsite_ref, cell, system, row_ref, col_ref):
    eye = lax.broadcasted_iota(jnp.int32, (128, 128), 0) == lax.broadcasted_iota(jnp.int32, (128, 128), 1)
    for v in range(3):
        cols = slice(128 * v, 128 * (v + 1))
        real = system[v, cols, :] + (shift - onsite_ref[cell : cell + 1, cols])
        imag = system[3 + v, cols, :] + BROADENING
        real, imag = jnp.where(eye, real, 0.0), jnp.where(eye, imag, 0.0)
        for axis, ref in ((0, row_ref), (1, col_ref)):
            down_real = jnp.sum(real, axis=axis, keepdims=True)
            down_imag = jnp.sum(imag, axis=axis, keepdims=True)
            scale = 1.0 / (down_real * down_real + down_imag * down_imag)
            for t, part in enumerate((down_real * scale, -down_imag * scale)):
                if axis == 0:
                    ref[t : t + 1, cols] = part
                else:
                    ref[t, cols, :] = jnp.broadcast_to(part, (128, 128))


def scale_strip(system, row_ref, col_ref, base, left, right, row):
    rows = pl.ds(row, STRIP)
    down_real, down_imag = col_ref[0, rows, :], col_ref[1, rows, :]
    at = lax.broadcasted_iota(jnp.int32, (STRIP, 128), 0) + row
    for v in range(3):
        on = at == lax.broadcasted_iota(jnp.int32, (STRIP, 128), 1) + 128 * v
        across_real = row_ref[0:1, 128 * v : 128 * (v + 1)]
        across_imag = row_ref[1:2, 128 * v : 128 * (v + 1)]
        real = jnp.where(on, 0.0, system[v, rows, :])
        imag = jnp.where(on, 0.0, system[3 + v, rows, :])
        real, imag = real * across_real - imag * across_imag, real * across_imag + imag * across_real
        to_right(right, v, split(real), row, STRIP)
        to_right(right, 3 + v, split(imag), row, STRIP)
        real, imag = down_real * real - down_imag * imag, down_real * imag + down_imag * real
        to_left(left, v, split(real), rows)
        to_left(left, 3 + v, split(imag), rows)
        base[v, rows, :] = jnp.where(on, down_real, 0.0) - real
        base[3 + v, rows, :] = jnp.where(on, down_imag, 0.0) - imag


def green_kernel(
    energy_ref,
    shift_ref,
    onsite_ref,
    sigma_in_ref,
    hop_in_ref,
    coup_in_ref,
    out_to_ref,
    sigma_ref,
    out_ref,
    table_ref,
    order_ref,
    hot_ref,
    spread_ref,
    row_ref,
    col_ref,
    hop_ref,
    coup_ref,
    first_system,
    second_system,
    base,
    green,
    placed_hi,
    placed_lo,
    picked_hi,
    picked_lo,
    more_hi,
    more_lo,
    sems,
    *operands,
):
    duos = [(operands[2 * s], operands[2 * s + 1]) for s in range(len(operands) // 2)]
    left_a, left_b, left_v, left_u, right_a, right_b, right_v = duos
    hop_copy = pltpu.make_async_copy(hop_in_ref, hop_ref, sems.at[0])
    coup_copy = pltpu.make_async_copy(coup_in_ref, coup_ref, sems.at[1])
    sigma_copy = pltpu.make_async_copy(sigma_in_ref, sigma_ref, sems.at[2])
    sigma_copy.start()
    hop_copy.start()
    coup_copy.start()
    energy = energy_ref[0]
    placed = (placed_hi, placed_lo)
    first_picked, second_picked = (picked_hi, picked_lo), (more_hi, more_lo)
    fill_tables(shift_ref, table_ref)
    fill_order(order_ref)

    sigma_copy.wait()

    def place(step, carry):
        for k in range(TOGETHER):
            fill_hot(shift_ref, hot_ref, step * TOGETHER + k)
        place_groups(sigma_ref, hot_ref, spread_ref, placed, 0, step * TOGETHER, TOGETHER)
        return carry

    lax.fori_loop(0, GROUPS // TOGETHER, place, 0)
    hop_copy.wait()
    coup_copy.wait()
    for t in range(2):
        assemble(placed, hop_ref, first_system, 0, t)
    inverse_diagonal(energy, onsite_ref, 0, first_system, row_ref, col_ref)
    for strip in range(12):
        scale_strip(first_system, row_ref, col_ref, base, left_a, right_a, strip * STRIP)

    def coupling(step):
        place_groups(sigma_ref, hot_ref, spread_ref, placed, 1, 4 * step, 4)
        if step == 2:
            return
        turned = coup_ref[step].T
        for v in range(3):
            cols = slice(128 * v, 128 * (v + 1))
            to_right(right_v, 3 * step + v, split(coup_ref[step, :, cols]))
            to_left(left_v, 3 * step + v, split(turned[:, cols] if step == 0 else -turned[:, cols]))

    def second_term(tile, value):
        to_left(left_b, tile, split(value))
        base[tile] += value

    def first_green(tile, value):
        value = base[tile] - value
        green[tile] = value
        parts = split(value)
        to_left(left_a, tile, parts)
        to_right(right_b, tile, parts)

    product(left_a, right_a, second_term, coupling)
    product(
        left_b,
        right_a,
        first_green,
        lambda step: place_groups(sigma_ref, hot_ref, spread_ref, placed, 1, 12 + 4 * step, 4),
    )

    def adjoint(tile, value):
        parts = split(value)
        to_left(left_b, tile, parts)
        to_right(right_a, tile, parts)

    def second_assembled(step):
        if step < 2:
            assemble(placed, hop_ref, second_system, 1, step)

    product(left_v, right_b, adjoint, second_assembled)

    def fold(tile, value):
        second_system[tile] -= value

    product(left_b, right_v, fold)
    inverse_diagonal(energy, onsite_ref, 1, second_system, row_ref, col_ref)

    def scale(step):
        for strip in range(4 * step, 4 * step + 4):
            scale_strip(second_system, row_ref, col_ref, base, left_v, right_b, strip * STRIP)

    product(left_a, right_v, lambda tile, value: to_left(left_u, tile, split(value)), scale)
    product(left_v, right_b, second_term)

    def second_green(tile, value):
        value = base[tile] - value
        first_system[tile] = value
        to_right(right_v, tile, split(value))

    product(left_b, right_b, second_green)

    def pick_second(step):
        for half in range(2):
            pick_atoms(first_system, table_ref, second_picked, 32 * step + 16 * half)

    product(left_u, right_v, lambda tile, value: to_left(left_a, tile, split(value)), pick_second)
    def send(chunk):
        rows = slice(768 * chunk, 768 * (chunk + 1))
        return pltpu.make_async_copy(out_ref.at[rows], out_to_ref.at[rows], sems.at[3 + chunk])

    for chunk in range(3):
        rows = slice(128 * chunk, 128 * (chunk + 1))

        def through(tile, value, rows=rows):
            green[tile, rows, :] += value

        def beside(step, chunk=chunk):
            if step == 0:
                order_pairs(second_picked, order_ref, out_ref, 1, chunk)
            if chunk > 0:
                if step < 2:
                    pick_atoms(green, table_ref, first_picked, 32 * (chunk - 1) + 16 * step)
                else:
                    order_pairs(first_picked, order_ref, out_ref, 0, chunk - 1)

        product(left_a, right_a, through, beside, rows)
        if chunk > 0:
            send(chunk - 1).start()
    for half in range(2):
        pick_atoms(green, table_ref, first_picked, 64 + 16 * half)
    order_pairs(first_picked, order_ref, out_ref, 0, 2)
    send(2).start()
    for chunk in range(3):
        send(chunk).wait()


def vmem():
    return pl.BlockSpec(memory_space=pltpu.VMEM)


def smem():
    return pl.BlockSpec(memory_space=pltpu.SMEM)


def green_pairs(energy, neighbor_shift, onsite, sigma_rows, hopping, coupling):
    left = [pltpu.VMEM((ORB, DUO), BF16)] * 2
    right = [pltpu.VMEM((DUO, DUO), BF16)] * 2
    return pl.pallas_call(
        green_kernel,
        out_shape=jax.ShapeDtypeStruct((ROWS, 128), F32),
        in_specs=[smem()] + [vmem()] * 2 + [pl.BlockSpec(memory_space=pl.ANY)] * 3,
        out_specs=pl.BlockSpec(memory_space=pl.ANY),
        scratch_shapes=[
            pltpu.VMEM((ROWS, 128), F32),
            pltpu.VMEM((ROWS, 128), F32),
            pltpu.VMEM((3, ATOMS, 128), jnp.int32),
            pltpu.VMEM((512, 512), BF16),
            pltpu.VMEM((GROUPS, 128, 256), BF16),
            pltpu.VMEM((TOGETHER, 128, 128), F32),
            pltpu.VMEM((8, ORB), F32),
            pltpu.VMEM((2, ORB, 128), F32),
            pltpu.VMEM((4, ORB, ORB), F32),
            pltpu.VMEM((2, ORB, ORB), F32),
            pltpu.VMEM((TILES, ORB, 128), F32),
            pltpu.VMEM((TILES, ORB, 128), F32),
            pltpu.VMEM((TILES, ORB, 128), F32),
            pltpu.VMEM((TILES, ORB, 128), F32),
            pltpu.VMEM((4 * ORB, 512), BF16),
            pltpu.VMEM((4 * ORB, 512), BF16),
            *([pltpu.VMEM((3 * ATOMS, 512), BF16)] * 4),
            pltpu.SemaphoreType.DMA((6,)),
            *left,
            *left,
            *left,
            *left,
            *right,
            *right,
            *right,
        ],
        compiler_params=pltpu.CompilerParams(vmem_limit_bytes=56 * 2**20),
        name="green_pairs",
    )(energy, neighbor_shift.T, onsite, sigma_rows, hopping, coupling)


def convolve_kernel(shift_ref, phonon_ref, in_ref, out_ref):
    source_energy = iota(1) // 8
    momentum = iota(1) % 8
    tiles = []
    for m in range(MODES):
        pair = []
        for d in range(2):
            wide = jnp.concatenate([phonon_ref[m, d]] * 16, axis=1)
            pair.append(wide)
        tiles.append(pair)
    rows = []
    for energy in range(16):
        value = jnp.zeros((8, 128), F32)
        for m in range(MODES):
            value = value + jnp.where(source_energy == energy - shift_ref[m], tiles[m][0], 0.0)
            value = value + jnp.where(source_energy == energy + shift_ref[m], tiles[m][1], 0.0)
        rows.append(value)
    kernel = jnp.concatenate(rows, axis=0)
    kernel_hi = kernel.astype(BF16)
    kernel_lo = (kernel - kernel_hi.astype(F32)).astype(BF16)
    for s in range(0, 18, 2):
        value = jnp.concatenate(
            [in_ref[pl.ds(s + k, 128, stride=18), :] for k in range(2)], axis=1
        )
        hi = value.astype(BF16)
        lo = (value - hi.astype(F32)).astype(BF16)
        total = jnp.dot(kernel_hi, hi, preferred_element_type=F32)
        total = total + jnp.dot(kernel_lo, hi, preferred_element_type=F32)
        total = total + jnp.dot(kernel_hi, lo, preferred_element_type=F32)
        for k in range(2):
            out_ref[pl.ds(s + k, 128, stride=18), :] = total[:, 128 * k : 128 * (k + 1)]


def convolve(mode_shift, phonon_kernel, rows):
    return pl.pallas_call(
        convolve_kernel,
        out_shape=jax.ShapeDtypeStruct((ROWS, 128), F32),
        in_specs=[smem(), vmem(), vmem()],
        out_specs=vmem(),
        compiler_params=pltpu.CompilerParams(vmem_limit_bytes=32 * 2**20),
        name="convolve",
    )(mode_shift, phonon_kernel, rows)


def rows_of(sigma):
    return sigma.reshape(2, PAIR_COLS // 128, 128).transpose(1, 0, 2).reshape(ROWS, 128)


def exchange(parts):
    return lax.all_to_all(parts, ("energy", "momentum"), split_axis=0, concat_axis=0, tiled=True)


def to_parts(rows):
    return rows.reshape(128, 9, 2, 128)


def body(hopping, coupling, onsite, sigma_in, neighbor_shift, mode_shift, phonon_kernel):
    energies = lax.axis_size("energy")
    energy = 2.0 * (lax.axis_index("energy").astype(F32) + 0.5) / energies
    pairs = green_pairs(
        energy.reshape(1),
        neighbor_shift,
        onsite,
        rows_of(sigma_in),
        hopping.reshape(4, ORB, ORB),
        coupling.reshape(2, ORB, ORB),
    )
    convolved = convolve(mode_shift, phonon_kernel, exchange(to_parts(pairs)).reshape(ROWS, 128))
    parts = convolved.reshape(128, 9, 2, 128).transpose(2, 0, 1, 3)
    moved = lax.all_to_all(parts, ("energy", "momentum"), split_axis=1, concat_axis=1, tiled=True)
    return moved.reshape(1, 1, 2, PAIR_COLS)


def solution(mesh):
    return jax.shard_map(
        body,
        mesh=mesh,
        in_specs=(
            P("momentum", None, None, None, None),
            P("momentum", None, None, None),
            P(),
            P("energy", "momentum", None, None),
            P(),
            P(),
            P(),
        ),
        out_specs=P("energy", "momentum", None, None),
        check_vma=False,
    )
```
